128 devices in a mesh: row: 16 (over y, x), col: 8 (over z, core).
Axes of the slice: x: 4, y: 4, z: 4, core: 2. Of those that a mesh axis runs over, the one named last changes fastest.
Arguments:
- amplitudes: bfloat16 [192, 128, 1024], P('row', 'col'), may hold values from -6 to 6
- hole_int: bfloat16 [192, 192, 128, 128], P('row', None, 'col'), may hold values from -0.109375 to 0.109375
- ladder_int: bfloat16 [1024, 1024], replicated, may hold values from -0.5 to 0.5
- cycle_virt: bfloat16 [1024, 1024], replicated, may hold values from -0.5 to 0.5
- cycle_occ: bfloat16 [128, 128], replicated, may hold values from -0.5 to 0.5
- irrep_rows: int32 [192], replicated, may hold values from 0 to 7
- irrep_cols: int32 [128], replicated, may hold values from 0 to 7
- irrep_virt: int32 [1024], replicated, may hold values from 0 to 7
Outputs:
- residual: bfloat16 [192, 128, 1024], P('row', 'col')
The draws below stay inside these ranges and needn't reach their ends.
All inputs are finite; a program needn't handle non-finite values.
Results may differ from the reference program's by a relative error of at most 0.014.
Values may be sent and summed in bfloat16 or wider, within the bound.
A program may use at most 128 MiB of HBM per device.

```python
import jax
import jax.numpy as jnp
from jax import lax

NV = 1024
OJ = 128
OI = 192
N_COL = 8


def set_ends(array, rng, least, high):
    shape = array.shape
    spot = [jax.random.randint(jax.random.fold_in(rng, axis), (), 0, shape[axis]) for axis in range(len(shape))]
    array = array.at[tuple(spot)].set(least)
    longest = shape.index(max(shape))
    spot[longest] = (spot[longest] + 1) % shape[longest]
    return array.at[tuple(spot)].set(high)


def block_levels(stream_key, shape, pieces, smallest, largest):
    loudness = 1.0
    for position, blocks in pieces:
        steps = jax.random.uniform(jax.random.fold_in(jax.random.fold_in(stream_key, 6), position), (blocks,), jnp.float32, smallest / len(pieces), largest / len(pieces))
        loudness = loudness * jnp.repeat(jnp.exp(steps), shape[position] // blocks).reshape((-1,) + (1,) * (len(shape) - 1 - position))
    return loudness


def normal_values(own_key, shape, scale, reach, shards=(), held_as=jnp.bfloat16):
    array = jax.random.normal(own_key, shape, jnp.float32) * scale
    if len(shards) > 0:
        array = block_levels(own_key, shape, shards, -0.22, 0.18) * array
    return jnp.clip(array, min=-reach, max=reach).astype(held_as)


def setup_inputs(seed: int = 0) -> dict:
    splits = jax.random.split(jax.random.key(seed), 9)
    amplitudes = normal_values(splits[0], (OI, OJ, NV), 1.0, 6.0, ((0, 16), (1, 8)))
    hole_int = normal_values(splits[1], (OI, OI, OJ, OJ), (OI * OJ // 8) ** -0.5, 0.109375, ((0, 16), (2, 8)))
    ladder_int = normal_values(splits[2], (NV, NV), (NV // 8) ** -0.5, 0.5)
    cycle_virt = normal_values(splits[3], (NV, NV), (NV // 8) ** -0.5, 0.5)
    cycle_occ = normal_values(splits[4], (OJ, OJ), OJ ** -0.5, 0.5)
    irrep_rows = set_ends(jax.random.randint(splits[5], (OI,), 0, 8), jax.random.fold_in(splits[5], 1), 0, 7).astype(jnp.int32)
    irrep_cols = set_ends(jax.random.randint(splits[6], (OJ,), 0, 8), jax.random.fold_in(splits[6], 1), 0, 7).astype(jnp.int32)
    irrep_virt = set_ends(jax.random.randint(splits[7], (NV,), 0, 8), jax.random.fold_in(splits[7], 1), 0, 7).astype(jnp.int32)
    return dict(amplitudes=amplitudes, hole_int=hole_int, ladder_int=ladder_int, cycle_virt=cycle_virt, cycle_occ=cycle_occ, irrep_rows=irrep_rows, irrep_cols=irrep_cols, irrep_virt=irrep_virt)


def reference(amplitudes, hole_int, ladder_int, cycle_virt, cycle_occ, irrep_rows, irrep_cols, irrep_virt):
    sym = jnp.bitwise_xor(irrep_rows[:, None], irrep_cols[None, :])
    amp_float = amplitudes.astype(jnp.float32)
    block_cols = OJ // N_COL
    amp_blocks = amp_float.reshape(OI, N_COL, block_cols, NV)

    def hole_row(args):
        int_row, sym_row = args
        keep = sym[:, :, None] == sym_row[None, None, :]
        masked = jnp.where(keep, int_row.astype(jnp.float32), jnp.float32(0.0))
        masked = masked.reshape(OI, N_COL, block_cols, OJ)
        parts = jnp.einsum('kclj,kcla->cja', masked, amp_blocks)
        parts = parts.astype(jnp.bfloat16).astype(jnp.float32)
        return jnp.sum(parts, axis=0)

    hole = lax.map(hole_row, (hole_int, sym))
    same_irrep = irrep_virt[:, None] == irrep_virt[None, :]
    zero = jnp.zeros((), jnp.bfloat16)
    flat_amp = amplitudes.reshape(-1, NV)
    onebody = jnp.dot(flat_amp, jnp.where(same_irrep, ladder_int, zero), preferred_element_type=jnp.float32)
    middle = jnp.dot(flat_amp, jnp.where(same_irrep, cycle_virt, zero), preferred_element_type=jnp.float32)
    middle = middle.astype(jnp.bfloat16).reshape(amplitudes.shape)
    cycle_term = jnp.einsum('jl,ila->ija', cycle_occ.astype(jnp.float32), middle.astype(jnp.float32)).astype(jnp.bfloat16)
    total = hole + onebody.reshape(hole.shape) + cycle_term.astype(jnp.float32)
    return total.astype(jnp.bfloat16)
```

```python
import functools

import jax
import jax.numpy as jnp
from jax import lax
from jax.experimental import pallas as pl
from jax.experimental.pallas import tpu as pltpu
from jax.sharding import PartitionSpec as P

MESH = pl.DeviceIdType.MESH
BF, F32 = jnp.bfloat16, jnp.float32
SIDE = 4
ROWS, COLS, VIRT = 12, 16, 1024
OCC_I, OCC_J = 192, 128
HALF = ROWS * COLS // 2
PAIR = 2 * SIDE * HALF
WIDTHS = (256, 256, 256, 256)
STARTS = tuple(sum(WIDTHS[:c]) for c in range(len(WIDTHS)))
NCH = len(WIDTHS)
MT = 512
KINDS = 8


def kernel(t_hbm, x_hbm, f_hbm, u_hbm, z_ref, rows_s, cols_v, virt_v, out_hbm,
           tv, xraw, xt, fv, uv, dk, cs, vcol, bd, mid, ob, outv, *rest):
    n = NCH
    ts, accs, s1s, r1s, s2s, r2s, fins = (rest[i * n:(i + 1) * n] for i in range(7))
    (tsem, tvsem, xsem, fusem, osem, gs, gr, as_, ar, bs, br) = rest[7 * n:]
    row, col = lax.axis_index("row"), lax.axis_index("col")
    y, x = row // SIDE, row % SIDE
    z, core = col // 2, col % 2

    def axes(h):
        return (y, x) if h == 0 else (x, y)

    def dev(h, p, q):
        p, q = p % SIDE, q % SIDE
        return {"row": q * SIDE + p if h == 0 else p * SIDE + q, "col": col}

    def owner(h, g, m):
        return g * SIDE + m if h == 0 else m * SIDE + g

    zdev = lambda d: {"row": row, "col": (z + d) % SIDE * 2 + core}
    sibling = {"row": row, "col": col + 1 - 2 * core}

    tcopies = []
    for c in range(n):
        for h in range(2):
            q, p = axes(h)
            cp = pltpu.make_async_copy(
                t_hbm.at[pl.ds(h * HALF, HALF), pl.ds(STARTS[c], WIDTHS[c])], ts[c].at[h, q, p], tsem.at[c * 2 + h])
            cp.start()
            tcopies.append(cp)

    bar = pltpu.get_barrier_semaphore()
    for h in range(2):
        q, p = axes(h)
        for d in (1, 3):
            pl.semaphore_signal(bar, inc=1, device_id=dev(h, p + d, q), device_id_type=MESH)
    pl.semaphore_signal(bar, inc=1, device_id=sibling, device_id_type=MESH)
    for d in (1, 2, 3):
        pl.semaphore_signal(bar, inc=1, device_id=zdev(d), device_id_type=MESH)

    tvcopy = pltpu.make_async_copy(t_hbm, tv, tvsem.at[0])
    tvcopy.start()
    xcopies = {}
    for first in (True, False):
        for h in range(2):
            for o in range(2):
                q, _ = axes(h)
                pr = q // 2 if first else 1 - q // 2
                g = pr * 2 + o
                for m in range(SIDE):
                    r = owner(h, g, m)
                    cp = pltpu.make_async_copy(
                        x_hbm.at[:, pl.ds(r * 2 * HALF + h * HALF, HALF), :], xraw.at[h, g, :, m],
                        xsem.at[((first * 2 + h) * 2 + o) * SIDE + m])
                    cp.start()
                    xcopies[first, h, o, m] = cp
        if first:
            ucopy = pltpu.make_async_copy(u_hbm, uv, fusem.at[1])
            ucopy.start()
    fcopy = pltpu.make_async_copy(f_hbm, fv, fusem.at[0])
    fcopy.start()
    for cp in tcopies:
        cp.wait()
    pl.semaphore_wait(bar, 8)

    sends = []

    def rc(c, h, kind, d, ref):
        q, p = axes(h)
        s = 1 if d == 0 else 3
        to = dev(h, p + s, q) if kind < 2 else dev(h, p, q + s)
        i = ((c * 2 + h) * KINDS + kind) * 2 + d
        return pltpu.make_async_remote_copy(
            src_ref=ref, dst_ref=ref, send_sem=gs.at[i], recv_sem=gr.at[i], device_id=to, device_id_type=MESH)

    def send(*a):
        cp = rc(*a)
        cp.start()
        sends.append(cp)

    def wait(*a):
        rc(*a).wait_recv()

    OFF = {2: 0, 3: 3, 4: 1, 5: 2}
    FW = {0: (2, 4), 1: (3, 5)}

    def src(v, d):
        return (v + (3 if d == 0 else 1)) % SIDE

    def S(c):
        for kind in (0, 2):
            for h in range(2):
                q, p = axes(h)
                for d in range(2):
                    send(c, h, kind, d, ts[c].at[h, q, p])

    def E1(c):
        for h in range(2):
            q, p = axes(h)
            for d in range(2):
                r = src(p, d)
                wait(c, h, 0, d, ts[c].at[h, q, r])
                send(c, h, 1, d, ts[c].at[h, q, r, pl.ds(HALF // 2 * d, HALF // 2)])
        for h in range(2):
            q, p = axes(h)
            for k in (4, 3):
                for d in range(2):
                    send(c, h, k, d, ts[c].at[h, q, (p + OFF[k]) % SIDE])

    def E2(c):
        for h in range(2):
            q, p = axes(h)
            for d in range(2):
                wait(c, h, 1, d, ts[c].at[h, q, (p + 2) % SIDE, pl.ds(HALF // 2 * d, HALF // 2)])
            for d in range(2):
                send(c, h, 5, d, ts[c].at[h, q, (p + 2) % SIDE])

    def G(c, ks):
        for k in ks:
            for h in range(2):
                q, p = axes(h)
                for d in range(2):
                    r, m = src(q, d), (p + OFF[k]) % SIDE
                    wait(c, h, k, d, ts[c].at[h, r, m])
                    if k in FW[d]:
                        send(c, h, 6 + FW[d].index(k), d, ts[c].at[h, r, m])

    def H(c):
        for f in range(2):
            for h in range(2):
                q, p = axes(h)
                for d in range(2):
                    wait(c, h, 6 + f, d, ts[c].at[h, (q + 2) % SIDE, (p + OFF[FW[d][f]]) % SIDE])

    def prep():
        row_c = cols_v[...]
        cs[...] = jnp.broadcast_to(row_c, (OCC_J, OCC_J)).T
        base = cs[pl.ds(pl.multiple_of(col * COLS, COLS), COLS), :] ^ jnp.broadcast_to(row_c, (COLS, OCC_J))
        for h in range(2):
            def body(b, _, h=h):
                r = owner(h, b // SIDE, b % SIDE)
                for kk in range(ROWS // 2):
                    v = base ^ rows_s[r * ROWS + h * (ROWS // 2) + kk]
                    dk[h, b // SIDE, b % SIDE, kk * COLS:(kk + 1) * COLS, :] = v.astype(F32).astype(BF)
                return 0
            lax.fori_loop(0, SIDE * SIDE, body, 0)
        lane = lax.broadcasted_iota(jnp.int32, (OCC_J, ROWS * COLS), 1)
        sub = lax.broadcasted_iota(jnp.int32, (OCC_J, ROWS * COLS), 0)
        pick = jnp.where(sub == col * COLS + (lane & (COLS - 1)), 1.0, 0.0).astype(BF)
        tiled = jnp.dot(z_ref[...], pick, preferred_element_type=F32)
        for i in range(ROWS):
            bd[i * OCC_J:(i + 1) * OCC_J, :] = jnp.where((lane >> 4) == i, tiled, 0.0).astype(BF)
        for b in range(VIRT // 128):
            piece = virt_v[:, b * 128:(b + 1) * 128].astype(F32)
            vcol[b * 128:(b + 1) * 128, :] = jnp.broadcast_to(piece, (128, 128)).T.astype(BF)

    def build(first):
        for h in range(2):
            q, _ = axes(h)
            pr = q // 2 if first else 1 - q // 2
            for o in range(2):
                for m in range(SIDE):
                    xcopies[first, h, o, m].wait()
        def body(b, _):
            h, o = b // 2, b % 2
            q = y + h * (x - y)
            pr = q // 2 if first else 1 - q // 2
            g = pr * 2 + o
            start = pl.multiple_of((h * SIDE + g) * SIDE * HALF, SIDE * HALF)
            for i in range(ROWS):
                xs = xraw[h, g, i].reshape(SIDE * HALF, OCC_J)
                keep = dk[h, g].reshape(SIDE * HALF, OCC_J) == rows_s[row * ROWS + i].astype(F32).astype(BF)
                xs = jnp.where(keep, xs, jnp.zeros((), BF))
                xt[i * OCC_J:(i + 1) * OCC_J, pl.ds(start, SIDE * HALF)] = xs.T
            return 0
        lax.fori_loop(0, 4, body, 0)

    def mask_virt(w):
        def body(b, _):
            rows = pl.ds(pl.multiple_of(b * 128, 128), 128)
            for j in range(VIRT // 128):
                lanes = slice(j * 128, (j + 1) * 128)
                keep = vcol[rows, :] == virt_v[:, lanes].astype(F32).astype(BF)
                w[rows, lanes] = jnp.where(keep, w[rows, lanes], jnp.zeros((), BF))
            return 0
        lax.fori_loop(0, VIRT // 128, body, 0)

    def middle():
        ucopy.wait()
        tvcopy.wait()
        mask_virt(uv)
        def body(b, _):
            lanes = pl.ds(pl.multiple_of(b * 256, 256), 256)
            mid[:, lanes] = jnp.dot(tv[...], uv[:, lanes], preferred_element_type=F32).astype(BF)
            return 0
        lax.fori_loop(0, VIRT // 256, body, 0)

    def onebody():
        fcopy.wait()
        mask_virt(fv)
        def body(b, _):
            lanes = pl.ds(pl.multiple_of(b * 256, 256), 256)
            ob[:, lanes] = jnp.dot(tv[...], fv[:, lanes], preferred_element_type=F32)
            return 0
        lax.fori_loop(0, VIRT // 256, body, 0)

    def dots(c, first):
        w = WIDTHS[c]
        per = MT // OCC_J
        def body(mt, _):
            rows = pl.ds(pl.multiple_of(mt * MT, MT), MT)
            if first:
                total = jnp.dot(bd[rows, :], mid[:, STARTS[c]:STARTS[c] + w], preferred_element_type=F32)
            else:
                total = accs[c][pl.ds(mt * per, per)].reshape(MT, w)
            for h in range(2):
                q, _ = axes(h)
                pr = q // 2 if first else 1 - q // 2
                start = pl.multiple_of(h * 2 * PAIR + pr * PAIR, PAIR)
                block = ts[c][h, pl.ds(pr * 2, 2)].reshape(PAIR, w)
                total = total + jnp.dot(xt[rows, pl.ds(start, PAIR)], block, preferred_element_type=F32)
            accs[c][pl.ds(mt * per, per)] = total.reshape(per, SIDE, 2, COLS, w)
            return 0
        lax.fori_loop(0, ROWS * OCC_J // MT, body, 0)

    def to_sibling(c):
        return pltpu.make_async_remote_copy(
            src_ref=s1s[c], dst_ref=r1s[c], send_sem=as_.at[c], recv_sem=ar.at[c], device_id=sibling, device_id_type=MESH)

    def to_z(c, d):
        return pltpu.make_async_remote_copy(
            src_ref=s2s[c].at[d - 1], dst_ref=r2s[c].at[d - 1], send_sem=bs.at[c * 3 + d - 1], recv_sem=br.at[c * 3 + d - 1],
            device_id=zdev(d), device_id_type=MESH)

    def SA(c):
        s1s[c][...] = accs[c][:, :, 1 - core].astype(BF)
        to_sibling(c).start()

    def SB(c):
        w = WIDTHS[c]
        to_sibling(c).wait_recv()
        for d in (2, 1, 3):
            to = (z + d) % SIDE
            s2s[c][d - 1] = (accs[c][:, to, core] + r1s[c][:, to].astype(F32)).astype(BF)
            to_z(c, d).start()
        one = ob[:, STARTS[c]:STARTS[c] + w].reshape(ROWS, COLS, w)
        fins[c][...] = accs[c][:, z, core] + r1s[c][:, z].astype(F32) + one

    def out_copy(c):
        cols = pl.ds(STARTS[c], WIDTHS[c])
        return pltpu.make_async_copy(outv.at[:, :, cols], out_hbm.at[:, :, cols], osem.at[c])

    def SC(c):
        w = WIDTHS[c]
        for d in (1, 3, 2):
            to_z(c, d).wait_recv()
        total = fins[c][...]
        for d in (1, 2, 3):
            total = total + r2s[c][d - 1].astype(F32)
        outv[:, :, STARTS[c]:STARTS[c] + w] = total.astype(BF)
        out_copy(c).start()

    S(0); S(1)
    prep()
    build(True)
    E1(0); G(0, (2,))
    middle()
    E2(0); S(2); E1(1)
    build(False)
    G(0, (3, 4, 5)); E2(1); G(1, (2,))
    onebody()
    S(3); E1(2)
    dots(0, True)
    H(0); G(1, (3, 4, 5)); E2(2); G(2, (2,))
    dots(0, False); SA(0)
    E1(3)
    dots(1, True)
    H(1); G(2, (3, 4, 5)); E2(3); G(3, (2,))
    SB(0)
    dots(1, False); SA(1)
    dots(2, True)
    H(2); G(3, (3, 4, 5))
    SB(1)
    dots(2, False); SA(2)
    dots(3, True)
    SC(0); SB(2)
    H(3)
    dots(3, False); SA(3)
    SC(1); SB(3); SC(2); SC(3)
    for cp in sends:
        cp.wait_send()
    for c in range(n):
        to_sibling(c).wait_send()
        for d in (1, 2, 3):
            to_z(c, d).wait_send()
        out_copy(c).wait()


def local(amplitudes, hole_int, ladder_int, cycle_virt, cycle_occ, irrep_rows, irrep_cols, irrep_virt):
    vm, dma = pltpu.VMEM, pltpu.SemaphoreType.DMA
    any_, vspec = pl.BlockSpec(memory_space=pl.ANY), pl.BlockSpec(memory_space=pltpu.VMEM)
    scratch = [
        vm((ROWS * COLS, VIRT), BF), vm((2, SIDE, ROWS, SIDE, HALF, OCC_J), BF), vm((ROWS * OCC_J, OCC_I * COLS), BF),
        vm((VIRT, VIRT), BF), vm((VIRT, VIRT), BF), vm((2, SIDE, SIDE, HALF, OCC_J), BF), vm((OCC_J, OCC_J), jnp.int32),
        vm((VIRT, 128), BF), vm((ROWS * OCC_J, ROWS * COLS), BF), vm((ROWS * COLS, VIRT), BF), vm((ROWS * COLS, VIRT), F32),
        vm((ROWS, COLS, VIRT), BF),
    ]
    scratch += [vm((2, SIDE, SIDE, HALF, w), BF) for w in WIDTHS]
    scratch += [vm((ROWS, SIDE, 2, COLS, w), F32) for w in WIDTHS]
    scratch += [vm((ROWS, SIDE, COLS, w), BF) for w in WIDTHS]
    scratch += [vm((ROWS, SIDE, COLS, w), BF) for w in WIDTHS]
    scratch += [vm((SIDE - 1, ROWS, COLS, w), BF) for w in WIDTHS]
    scratch += [vm((SIDE - 1, ROWS, COLS, w), BF) for w in WIDTHS]
    scratch += [vm((ROWS, COLS, w), F32) for w in WIDTHS]
    ng = NCH * 2 * KINDS * 2
    scratch += [dma((NCH * 2,)), dma((1,)), dma((32,)), dma((2,)), dma((NCH,)), dma((ng,)), dma((ng,)),
                dma((NCH,)), dma((NCH,)), dma((NCH * 3,)), dma((NCH * 3,))]
    return pl.pallas_call(
        kernel,
        out_shape=jax.ShapeDtypeStruct((ROWS, COLS, VIRT), BF),
        in_specs=[any_, any_, any_, any_, vspec, pl.BlockSpec(memory_space=pltpu.SMEM), vspec, vspec],
        out_specs=any_,
        scratch_shapes=scratch,
        compiler_params=pltpu.CompilerParams(collective_id=0, has_side_effects=True, vmem_limit_bytes=60 * 2**20),
        name="residual",
    )(amplitudes.reshape(ROWS * COLS, VIRT), hole_int.reshape(ROWS, OCC_I * COLS, OCC_J), ladder_int, cycle_virt,
      cycle_occ, irrep_rows, irrep_cols.reshape(1, OCC_J), irrep_virt.reshape(1, VIRT))


def solution(mesh):
    placed = (P("row", "col", None), P("row", None, "col", None), P(), P(), P(), P(), P(), P())
    return jax.shard_map(
        local, mesh=mesh, in_specs=placed, out_specs=P("row", "col", None), check_vma=False
    )
```

```python
import functools

import jax
import jax.numpy as jnp
from jax import lax
from jax.experimental import pallas as pl
from jax.experimental.pallas import tpu as pltpu
from jax.sharding import PartitionSpec as P

MESH = pl.DeviceIdType.MESH
BF, F32 = jnp.bfloat16, jnp.float32
SIDE = 4
ROWS, COLS, VIRT = 12, 16, 1024
OCC_I, OCC_J = 192, 128
HALF = ROWS * COLS // 2
WIDTHS = (256, 256, 256, 256)
STARTS = tuple(sum(WIDTHS[:c]) for c in range(len(WIDTHS)))
NCH = len(WIDTHS)
PARTS = (1, 1, 1, 2)
MT = 768
EVENTS = 8


SCHEDULE = (
    ('S', 0), ('S', 1), ('S', 2), ('prep',), ('build', True), ('E1', 0), ('G', 0, 2), ('onebody',), ('E1', 2), ('E2', 0), ('middle',), ('E1', 1), ('build', False), ('E2', 2), ('G', 0, 3, 4, 5), ('E2', 1), ('S', 3), ('G', 2, 2), ('dots', 0, 0), ('G', 2, 3, 4, 5), ('G', 1, 2), ('dots', 2, 0), ('G', 1, 3, 4, 5), ('dots', 1, 0), ('H', 0), ('E1', 3), ('dots', 0, 1), ('SA', 0), ('H', 2), ('dots', 2, 1), ('SA', 2), ('E2', 3), ('SB', 0), ('H', 1), ('dots', 1, 1), ('SA', 1), ('G', 3, 2), ('G', 3, 3, 4, 5), ('SB', 2), ('dots', 3, 0), ('SB', 1), ('dots', 3, 2), ('H', 3), ('dots', 3, 3, 0), ('SA', 3, 0), ('dots', 3, 3, 1), ('SA', 3, 1), ('SB', 3, 0), ('SB', 3, 1),
)


def kernel(t_hbm, x_hbm, f_hbm, u_hbm, z_hbm, rows_hbm, cols_hbm, virt_hbm, fin_hbm, r2_hbm,
           tv, xraw, xt, fv, uv, dk, cs, vcol, bd, mid, ob, finv, z_ref, cols_v, virt_v, rows_s, *rest):
    n = NCH
    ts, accs, s1s, r1s, s2s = (rest[i * n:(i + 1) * n] for i in range(5))
    (tsem, tvsem, xsem, fusem, osem, smsem, gs, gr, as_, ar, bs, br) = rest[5 * n:]
    row, col = lax.axis_index("row"), lax.axis_index("col")
    y, x = row // SIDE, row % SIDE
    z, core = col // 2, col % 2

    def axes(h):
        return (y, x) if h == 0 else (x, y)

    def dev(h, p, q):
        p, q = p % SIDE, q % SIDE
        return {"row": q * SIDE + p if h == 0 else p * SIDE + q, "col": col}

    def owner(h, g, m):
        return g * SIDE + m if h == 0 else m * SIDE + g

    zdev = lambda d: {"row": row, "col": (z + d) % SIDE * 2 + core}
    sibling = {"row": row, "col": col + 1 - 2 * core}

    small = []
    for i, (a, b) in enumerate(((rows_hbm, rows_s), (cols_hbm, cols_v), (z_hbm, z_ref), (virt_hbm, virt_v))):
        cp = pltpu.make_async_copy(a, b, smsem.at[i])
        small.append(cp)

    def block(h, g, m):
        return (h * SIDE + g) * SIDE + m

    for c in range(n):
        for h in range(2):
            q, p = axes(h)
            pltpu.make_async_copy(
                t_hbm.at[pl.ds(h * HALF, HALF), pl.ds(STARTS[c], WIDTHS[c])], ts[c].at[block(h, q, p)], tsem.at[0]).start()

    bar = pltpu.get_barrier_semaphore()
    for h in range(2):
        q, p = axes(h)
        for d in (1, 3):
            pl.semaphore_signal(bar, inc=1, device_id=dev(h, p + d, q), device_id_type=MESH)
    pl.semaphore_signal(bar, inc=1, device_id=sibling, device_id_type=MESH)
    for d in (1, 2, 3):
        pl.semaphore_signal(bar, inc=1, device_id=zdev(d), device_id_type=MESH)

    for cp in small:
        cp.start()
    tvcopy = pltpu.make_async_copy(t_hbm, tv, tvsem.at[0])
    tvcopy.start()
    ucopy = pltpu.make_async_copy(u_hbm, uv, fusem.at[1])
    fcopy = pltpu.make_async_copy(f_hbm, fv, fusem.at[0])
    for first in (True, False):
        for h in range(2):
            for o in range(2):
                q, _ = axes(h)
                g = (q // 2 if first else 1 - q // 2) * 2 + o
                for m in range(SIDE):
                    r = owner(h, g, m)
                    pltpu.make_async_copy(
                        x_hbm.at[:, pl.ds(r * 2 * HALF + h * HALF, HALF), :], xraw.at[h, g, :, m], xsem.at[1 - first]).start()
        if first:
            ucopy.start()
    fcopy.start()
    pltpu.make_async_copy(t_hbm, tv, tsem.at[0]).wait()
    pl.semaphore_wait(bar, 8)

    def send(c, h, kind, d, ref):
        q, p = axes(h)
        s = 1 if d == 0 else 3
        to = dev(h, p + s, q) if kind < 2 else dev(h, p, q + s)
        pltpu.make_async_remote_copy(
            src_ref=ref, dst_ref=ref, send_sem=gs.at[c], recv_sem=gr.at[c * EVENTS + kind], device_id=to,
            device_id_type=MESH).start()

    def arrived(c, kind, blocks):
        ref = ts[c].at[pl.ds(0, blocks)]
        pltpu.make_async_remote_copy(
            src_ref=ref, dst_ref=ref, send_sem=gs.at[c], recv_sem=gr.at[c * EVENTS + kind], device_id=sibling,
            device_id_type=MESH).wait_recv()

    OFF = {2: 0, 3: 3, 4: 1, 5: 2}
    FW = {0: (2, 4), 1: (3, 5)}

    def src(v, d):
        return (v + (3 if d == 0 else 1)) % SIDE

    def S(c):
        for kind in (0, 2):
            for h in range(2):
                q, p = axes(h)
                for d in range(2):
                    send(c, h, kind, d, ts[c].at[block(h, q, p)])

    def E1(c):
        arrived(c, 0, 4)
        for h in range(2):
            q, p = axes(h)
            for d in range(2):
                send(c, h, 1, d, ts[c].at[block(h, q, src(p, d)), pl.ds(HALF // 2 * d, HALF // 2)])
        for k in range(2):
            for h in range(2):
                q, p = axes(h)
                for d in range(2):
                    kind = (4, 3)[k ^ d]
                    send(c, h, kind, d, ts[c].at[block(h, q, (p + OFF[kind]) % SIDE)])

    def E2(c):
        arrived(c, 1, 2)
        for h in range(2):
            q, p = axes(h)
            for d in range(2):
                send(c, h, 5, d, ts[c].at[block(h, q, (p + 2) % SIDE)])

    def G(c, *ks):
        for k in ks or (2, 3, 4, 5):
            arrived(c, k, 4)
            d = 0 if k in FW[0] else 1
            for h in range(2):
                q, p = axes(h)
                send(c, h, 6 + FW[d].index(k), d, ts[c].at[block(h, src(q, d), (p + OFF[k]) % SIDE)])

    def H(c):
        arrived(c, 6, 4)
        arrived(c, 7, 4)

    def prep():
        small[1].wait()
        small[0].wait()
        row_c = cols_v[...]
        cs[...] = jnp.broadcast_to(row_c, (OCC_J, OCC_J)).T
        base = cs[pl.ds(pl.multiple_of(col * COLS, COLS), COLS), :] ^ jnp.broadcast_to(row_c, (COLS, OCC_J))
        for h in range(2):
            def body(b, _, h=h):
                r = owner(h, b // SIDE, b % SIDE)
                for kk in range(ROWS // 2):
                    v = base ^ rows_s[r * ROWS + h * (ROWS // 2) + kk]
                    dk[h, b // SIDE, b % SIDE, kk * COLS:(kk + 1) * COLS, :] = v.astype(F32).astype(BF)
                return 0
            lax.fori_loop(0, SIDE * SIDE, body, 0)
        small[2].wait()
        lane = lax.broadcasted_iota(jnp.int32, (OCC_J, ROWS * COLS), 1)
        sub = lax.broadcasted_iota(jnp.int32, (OCC_J, ROWS * COLS), 0)
        pick = jnp.where(sub == col * COLS + (lane & (COLS - 1)), 1.0, 0.0).astype(BF)
        tiled = jnp.dot(z_ref[...], pick, preferred_element_type=F32)
        for i in range(ROWS):
            bd[i * OCC_J:(i + 1) * OCC_J, :] = jnp.where((lane >> 4) == i, tiled, 0.0).astype(BF)
        small[3].wait()
        tvcopy.wait()
        for b in range(VIRT // 128):
            piece = virt_v[:, b * 128:(b + 1) * 128].astype(F32)
            vcol[b * 128:(b + 1) * 128, :] = jnp.broadcast_to(piece, (128, 128)).T.astype(BF)

    def build(first):
        pltpu.make_async_copy(x_hbm.at[pl.ds(0, ROWS // 2)], x_hbm.at[pl.ds(0, ROWS // 2)], xsem.at[1 - first]).wait()
        def body(b, _):
            h, o = b // 2, b % 2
            q = y + h * (x - y)
            pr = q // 2 if first else 1 - q // 2
            g = pr * 2 + o
            start = pl.multiple_of((h * SIDE + g) * SIDE * HALF, SIDE * HALF)
            for i in range(ROWS):
                xs = xraw[h, g, i].reshape(SIDE * HALF, OCC_J)
                keep = dk[h, g].reshape(SIDE * HALF, OCC_J) == rows_s[row * ROWS + i].astype(F32).astype(BF)
                xs = jnp.where(keep, xs, jnp.zeros((), BF))
                xt[i * OCC_J:(i + 1) * OCC_J, pl.ds(start, SIDE * HALF)] = xs.T
            return 0
        lax.fori_loop(0, 4, body, 0)

    def mask_virt(w):
        def body(b, _):
            rows = pl.ds(pl.multiple_of(b * 128, 128), 128)
            for j in range(VIRT // 128):
                lanes = slice(j * 128, (j + 1) * 128)
                keep = vcol[rows, :] == virt_v[:, lanes].astype(F32).astype(BF)
                w[rows, lanes] = jnp.where(keep, w[rows, lanes], jnp.zeros((), BF))
            return 0
        lax.fori_loop(0, VIRT // 128, body, 0)

    def middle():
        ucopy.wait()
        mask_virt(uv)
        def body(b, _):
            lanes = pl.ds(pl.multiple_of(b * 256, 256), 256)
            mid[:, lanes] = jnp.dot(tv[...], uv[:, lanes], preferred_element_type=F32).astype(BF)
            return 0
        lax.fori_loop(0, VIRT // 256, body, 0)

    def onebody():
        fcopy.wait()
        mask_virt(fv)
        def body(b, _):
            lanes = pl.ds(pl.multiple_of(b * 256, 256), 256)
            ob[:, lanes] = jnp.dot(tv[...], fv[:, lanes], preferred_element_type=F32)
            return 0
        lax.fori_loop(0, VIRT // 256, body, 0)

    def dots(c, groups, part=None):
        w = WIDTHS[c]
        per = MT // OCC_J

        def product(rows, h, start, count):
            ks = pl.ds(pl.multiple_of((h * SIDE + start) * SIDE * HALF, SIDE * HALF), count * SIDE * HALF)
            blocks = ts[c][pl.ds((h * SIDE + start) * SIDE, count * SIDE)].reshape(count * SIDE * HALF, w)
            return jnp.dot(xt[rows, ks], blocks, preferred_element_type=F32)

        def body(mt, _):
            rows = pl.ds(pl.multiple_of(mt * MT, MT), MT)
            if groups == 0:
                total = jnp.dot(bd[rows, :], mid[:, STARTS[c]:STARTS[c] + w], preferred_element_type=F32)
            else:
                total = accs[c][pl.ds(mt * per, per)].reshape(MT, w)
            for h in range(2):
                q, _ = axes(h)
                if groups < 2:
                    total = total + product(rows, h, (q // 2 if groups == 0 else 1 - q // 2) * 2, 2)
                else:
                    total = total + product(rows, h, 3 - q if groups == 2 else (q + 2) % SIDE, 1)
            accs[c][pl.ds(mt * per, per)] = total.reshape(per, SIDE, 2, COLS, w)
            return 0
        if part is None:
            lax.fori_loop(0, ROWS * OCC_J // MT, body, 0)
        else:
            body(part, 0)

    def share(c, part):
        size = ROWS // PARTS[c]
        return pl.ds(part * size, size)

    def to_sibling(c, part):
        i = share(c, part)
        return pltpu.make_async_remote_copy(
            src_ref=s1s[c].at[i], dst_ref=r1s[c].at[i], send_sem=as_.at[2 * c + part], recv_sem=ar.at[2 * c + part],
            device_id=sibling, device_id_type=MESH)

    def SA(c, part=0):
        i = share(c, part)
        s1s[c][i] = accs[c][i, :, 1 - core].astype(BF)
        to_sibling(c, part).start()

    def SB(c, part=0):
        w, i = WIDTHS[c], share(c, part)
        cols = pl.ds(STARTS[c], w)
        to_sibling(c, part).wait_recv()
        for d in (2, 1, 3):
            to = (z + d) % SIDE
            s2s[c][d - 1, i] = (accs[c][i, to, core] + r1s[c][i, to].astype(F32)).astype(BF)
            pltpu.make_async_remote_copy(
                src_ref=s2s[c].at[d - 1, i], dst_ref=r2_hbm.at[d - 1, i, :, cols], send_sem=bs.at[0], recv_sem=br.at[0],
                device_id=zdev(d), device_id_type=MESH).start()
        size = ROWS // PARTS[c]
        one = ob[part * size * COLS:(part + 1) * size * COLS, STARTS[c]:STARTS[c] + w].reshape(size, COLS, w)
        finv[i, :, cols] = accs[c][i, z, core] + r1s[c][i, z].astype(F32) + one
        pltpu.make_async_copy(finv.at[i, :, cols], fin_hbm.at[i, :, cols], osem.at[0]).start()

    for name, *args in SCHEDULE:
        dict(S=S, E1=E1, E2=E2, G=G, H=H, prep=prep, build=build, middle=middle, onebody=onebody, dots=dots, SA=SA, SB=SB)[name](*args)

    for c in range(n):
        ref = ts[c].at[pl.ds(0, 30)]
        pltpu.make_async_remote_copy(
            src_ref=ref, dst_ref=ref, send_sem=gs.at[c], recv_sem=gr.at[c], device_id=sibling, device_id_type=MESH).wait_send()
        for part in range(PARTS[c]):
            to_sibling(c, part).wait_send()
    pltpu.make_async_copy(finv, fin_hbm, osem.at[0]).wait()
    last = pltpu.make_async_remote_copy(
        src_ref=r2_hbm, dst_ref=r2_hbm, send_sem=bs.at[0], recv_sem=br.at[0], device_id=sibling, device_id_type=MESH)
    last.wait_send()
    last.wait_recv()


def local(amplitudes, hole_int, ladder_int, cycle_virt, cycle_occ, irrep_rows, irrep_cols, irrep_virt):
    vm, dma = pltpu.VMEM, pltpu.SemaphoreType.DMA
    any_ = pl.BlockSpec(memory_space=pl.ANY)
    scratch = [
        vm((ROWS * COLS, VIRT), BF), vm((2, SIDE, ROWS, SIDE, HALF, OCC_J), BF), vm((ROWS * OCC_J, OCC_I * COLS), BF),
        vm((VIRT, VIRT), BF), vm((VIRT, VIRT), BF), vm((2, SIDE, SIDE, HALF, OCC_J), BF), vm((OCC_J, OCC_J), jnp.int32),
        vm((VIRT, 128), BF), vm((ROWS * OCC_J, ROWS * COLS), BF), vm((ROWS * COLS, VIRT), BF), vm((ROWS * COLS, VIRT), F32),
        vm((ROWS, COLS, VIRT), F32), vm((OCC_J, OCC_J), BF), vm((1, OCC_J), jnp.int32), vm((1, VIRT), jnp.int32),
        pltpu.SMEM((OCC_I,), jnp.int32),
    ]
    scratch += [vm((2 * SIDE * SIDE, HALF, w), BF) for w in WIDTHS]
    scratch += [vm((ROWS, SIDE, 2, COLS, w), F32) for w in WIDTHS]
    scratch += [vm((ROWS, SIDE, COLS, w), BF) for w in WIDTHS]
    scratch += [vm((ROWS, SIDE, COLS, w), BF) for w in WIDTHS]
    scratch += [vm((SIDE - 1, ROWS, COLS, w), BF) for w in WIDTHS]
    scratch += [dma((k,)) for k in (1, 1, 2, 2, 1, 4, NCH, NCH * EVENTS, 2 * NCH, 2 * NCH, 1, 1)]
    own, others = pl.pallas_call(
        kernel,
        out_shape=(jax.ShapeDtypeStruct((ROWS, COLS, VIRT), F32), jax.ShapeDtypeStruct((SIDE - 1, ROWS, COLS, VIRT), BF)),
        in_specs=[any_] * 8,
        out_specs=(any_, any_),
        scratch_shapes=scratch,
        compiler_params=pltpu.CompilerParams(collective_id=0, has_side_effects=True, vmem_limit_bytes=60 * 2**20),
        name="residual",
    )(amplitudes.reshape(ROWS * COLS, VIRT), hole_int.reshape(ROWS, OCC_I * COLS, OCC_J), ladder_int, cycle_virt,
      cycle_occ, irrep_rows, irrep_cols.reshape(1, OCC_J), irrep_virt.reshape(1, VIRT))
    return (own + others[0].astype(F32) + others[1].astype(F32) + others[2].astype(F32)).astype(BF)


def solution(mesh):
    placed = (P("row", "col", None), P("row", None, "col", None), P(), P(), P(), P(), P(), P())
    return jax.shard_map(
        local, mesh=mesh, in_specs=placed, out_specs=P("row", "col", None), check_vma=False
    )
```

```python
import functools

import jax
import jax.numpy as jnp
from jax import lax
from jax.experimental import pallas as pl
from jax.experimental.pallas import tpu as pltpu
from jax.sharding import PartitionSpec as P

MESH = pl.DeviceIdType.MESH
BF, F32 = jnp.bfloat16, jnp.float32
SIDE = 4
ROWS, COLS, VIRT = 12, 16, 1024
OCC_I, OCC_J = 192, 128
HALF = ROWS * COLS // 2
WIDTHS = (256, 256, 256, 256)
STARTS = tuple(sum(WIDTHS[:c]) for c in range(len(WIDTHS)))
NCH = len(WIDTHS)
PARTS = (1, 1, 1, 4)
EVENTS = 8


SCHEDULE = (
    ('D1', 0), ('O', 0), ('D1', 1), ('D1', 2), ('prep',), ('build', True), ('E1', 0), ('D1', 3), ('N', 0), ('middle',), ('E1', 1), ('E2', 0), ('N', 1), ('build', False), ('O', 1), ('G', 0, 3), ('G', 0, 4), ('G', 0, 2), ('onebody',), ('G', 0, 5), ('E2', 1), ('E1', 2), ('dots', 0, 0), ('O', 2), ('G', 1, 2), ('N', 2), ('G', 1, 3), ('G', 1, 4), ('H', 0), ('dots', 0, 1), ('G', 1, 5), ('E2', 2), ('SA', 0), ('E1', 3), ('dots', 1, 0), ('N', 3), ('SB', 0), ('G', 2, 3), ('G', 2, 4), ('G', 2, 2), ('H', 1), ('dots', 1, 1), ('G', 2, 5), ('O', 3), ('SA', 1), ('E2', 3), ('dots', 2, 0), ('G', 3, 4), ('G', 3, 3), ('SB', 1), ('H', 2), ('dots', 2, 1), ('G', 3, 2), ('SA', 2), ('G', 3, 5), ('dots', 3, 0), ('SB', 2), ('dots', 3, 2), ('H', 3), ('dots', 3, 3, 0), ('SA', 3, 0), ('dots', 3, 3, 1), ('SA', 3, 1), ('dots', 3, 3, 2), ('SA', 3, 2), ('dots', 3, 3, 3), ('SA', 3, 3), ('SB', 3, 0), ('SB', 3, 1), ('SB', 3, 2), ('SB', 3, 3),
)


def kernel(t_hbm, x_hbm, f_hbm, u_hbm, z_hbm, rows_hbm, cols_hbm, virt_hbm, fin_hbm, r2_hbm,
           tv, xraw, xt, fv, uv, dk, cs, vcol, bd, mid, ob, finv, z_ref, cols_v, virt_v, rows_s, *rest):
    n = NCH
    ts, accs, s1s, r1s, s2s = (rest[i * n:(i + 1) * n] for i in range(5))
    (tsem, tvsem, xsem, fusem, osem, smsem, gs, gr, as_, ar, bs, br) = rest[5 * n:]
    row, col = lax.axis_index("row"), lax.axis_index("col")
    y, x = row // SIDE, row % SIDE
    z, core = col // 2, col % 2

    def axes(h):
        return (y, x) if h == 0 else (x, y)

    def dev(h, p, q):
        p, q = p % SIDE, q % SIDE
        return {"row": q * SIDE + p if h == 0 else p * SIDE + q, "col": col}

    def owner(h, g, m):
        return g * SIDE + m if h == 0 else m * SIDE + g

    zdev = lambda d: {"row": row, "col": (z + d) % SIDE * 2 + core}
    sibling = {"row": row, "col": col + 1 - 2 * core}

    small = []
    for i, (a, b) in enumerate(((rows_hbm, rows_s), (cols_hbm, cols_v), (z_hbm, z_ref), (virt_hbm, virt_v))):
        cp = pltpu.make_async_copy(a, b, smsem.at[i])
        small.append(cp)

    def block(h, g, m):
        return (h * SIDE + g) * SIDE + m

    bar = pltpu.get_barrier_semaphore()
    for h in range(2):
        q, p = axes(h)
        for d in (1, 3):
            pl.semaphore_signal(bar, inc=1, device_id=dev(h, p + d, q), device_id_type=MESH)
    pl.semaphore_signal(bar, inc=1, device_id=sibling, device_id_type=MESH)
    for d in (1, 2, 3):
        pl.semaphore_signal(bar, inc=1, device_id=zdev(d), device_id_type=MESH)

    tvcopy = pltpu.make_async_copy(t_hbm, tv, tvsem.at[0])
    ucopy = pltpu.make_async_copy(u_hbm, uv, fusem.at[1])
    fcopy = pltpu.make_async_copy(f_hbm, fv, fusem.at[0])

    def load():
        for c in range(n):
            for h in range(2):
                q, p = axes(h)
                pltpu.make_async_copy(
                    t_hbm.at[pl.ds(h * HALF, HALF), pl.ds(STARTS[c], WIDTHS[c])], ts[c].at[block(h, q, p)], tsem.at[0]).start()
        for cp in small:
            cp.start()
        tvcopy.start()
        for first in (True, False):
            for h in range(2):
                for o in range(2):
                    q, _ = axes(h)
                    g = (q // 2 if first else 1 - q // 2) * 2 + o
                    source = x_hbm.at[:, g, :, h] if h == 0 else x_hbm.at[:, :, g, h]
                    pltpu.make_async_copy(source, xraw.at[h, g], xsem.at[1 - first]).start()
            if first:
                ucopy.start()
        fcopy.start()

    load()
    pl.semaphore_wait(bar, 8)

    def send(c, h, kind, d, ref, source=None):
        q, p = axes(h)
        s = 1 if d == 0 else 3
        to = dev(h, p + s, q) if kind < 2 else dev(h, p, q + s)
        pltpu.make_async_remote_copy(
            src_ref=ref if source is None else source, dst_ref=ref, send_sem=gs.at[c],
            recv_sem=gr.at[c * EVENTS + kind], device_id=to,
            device_id_type=MESH).start()

    def arrived(c, kind, blocks):
        ref = ts[c].at[pl.ds(0, blocks)]
        pltpu.make_async_remote_copy(
            src_ref=ref, dst_ref=ref, send_sem=gs.at[c], recv_sem=gr.at[c * EVENTS + kind], device_id=sibling,
            device_id_type=MESH).wait_recv()

    OFF = {2: 0, 3: 3, 4: 1, 5: 2}
    FW = {0: (2, 4), 1: (3, 5)}

    def src(v, d):
        return (v + (3 if d == 0 else 1)) % SIDE

    def first_sends(c, kind):
        for h in range(2):
            q, p = axes(h)
            for d in range(2):
                send(c, h, kind, d, ts[c].at[block(h, q, p)],
                     t_hbm.at[pl.ds(h * HALF, HALF), pl.ds(STARTS[c], WIDTHS[c])])

    def D1(c):
        first_sends(c, 0)

    def O(c):
        first_sends(c, 2)

    def E1(c):
        arrived(c, 0, 4)
        for h in range(2):
            q, p = axes(h)
            for d in range(2):
                send(c, h, 1, d, ts[c].at[block(h, q, src(p, d)), pl.ds(HALF // 2 * d, HALF // 2)])

    def N(c):
        for k in range(2):
            for h in range(2):
                q, p = axes(h)
                for d in range(2):
                    kind = (4, 3)[k ^ d]
                    send(c, h, kind, d, ts[c].at[block(h, q, (p + OFF[kind]) % SIDE)])

    def E2(c):
        arrived(c, 1, 2)
        for h in range(2):
            q, p = axes(h)
            for d in range(2):
                send(c, h, 5, d, ts[c].at[block(h, q, (p + 2) % SIDE)])

    def G(c, *ks):
        for k in ks or (2, 3, 4, 5):
            arrived(c, k, 4)
            d = 0 if k in FW[0] else 1
            for h in range(2):
                q, p = axes(h)
                send(c, h, 6 + FW[d].index(k), d, ts[c].at[block(h, src(q, d), (p + OFF[k]) % SIDE)])

    def H(c):
        arrived(c, 6, 4)
        arrived(c, 7, 4)

    def prep():
        small[1].wait()
        small[0].wait()
        row_c = cols_v[...]
        cs[...] = jnp.broadcast_to(row_c, (OCC_J, OCC_J)).T
        base = cs[pl.ds(pl.multiple_of(col * COLS, COLS), COLS), :] ^ jnp.broadcast_to(row_c, (COLS, OCC_J))
        for h in range(2):
            def body(b, _, h=h):
                r = owner(h, b // SIDE, b % SIDE)
                for kk in range(ROWS // 2):
                    v = base ^ rows_s[r * ROWS + h * (ROWS // 2) + kk]
                    dk[h, b // SIDE, b % SIDE, kk * COLS:(kk + 1) * COLS, :] = v.astype(F32).astype(BF)
                return 0
            lax.fori_loop(0, SIDE * SIDE, body, 0)
        small[2].wait()
        lane = lax.broadcasted_iota(jnp.int32, (OCC_J, ROWS * COLS), 1)
        sub = lax.broadcasted_iota(jnp.int32, (OCC_J, ROWS * COLS), 0)
        pick = jnp.where(sub == col * COLS + (lane & (COLS - 1)), 1.0, 0.0).astype(BF)
        tiled = jnp.dot(z_ref[...], pick, preferred_element_type=F32)
        for i in range(ROWS):
            bd[i * OCC_J:(i + 1) * OCC_J, :] = jnp.where((lane >> 4) == i, tiled, 0.0).astype(BF)
        small[3].wait()
        tvcopy.wait()
        pltpu.make_async_copy(t_hbm, tv, tsem.at[0]).wait()
        for b in range(VIRT // 128):
            piece = virt_v[:, b * 128:(b + 1) * 128].astype(F32)
            vcol[b * 128:(b + 1) * 128, :] = jnp.broadcast_to(piece, (128, 128)).T.astype(BF)

    def build(first):
        pltpu.make_async_copy(xraw.at[0], xraw.at[0], xsem.at[1 - first]).wait()
        def body(b, _):
            h, o = b // 2, b % 2
            q = y + h * (x - y)
            pr = q // 2 if first else 1 - q // 2
            g = pr * 2 + o
            start = pl.multiple_of((h * SIDE + g) * SIDE * HALF, SIDE * HALF)
            for i in range(ROWS):
                xs = xraw[h, g, i].reshape(SIDE * HALF, OCC_J)
                keep = dk[h, g].reshape(SIDE * HALF, OCC_J) == rows_s[row * ROWS + i].astype(F32).astype(BF)
                xs = jnp.where(keep, xs, jnp.zeros((), BF))
                xt[i * OCC_J:(i + 1) * OCC_J, pl.ds(start, SIDE * HALF)] = xs.T
            return 0
        lax.fori_loop(0, 4, body, 0)

    def mask_virt(w):
        def body(b, _):
            rows = pl.ds(pl.multiple_of(b * 128, 128), 128)
            for j in range(VIRT // 128):
                lanes = slice(j * 128, (j + 1) * 128)
                keep = vcol[rows, :] == virt_v[:, lanes].astype(F32).astype(BF)
                w[rows, lanes] = jnp.where(keep, w[rows, lanes], jnp.zeros((), BF))
            return 0
        lax.fori_loop(0, VIRT // 128, body, 0)

    def middle():
        ucopy.wait()
        mask_virt(uv)
        def body(b, _):
            lanes = pl.ds(pl.multiple_of(b * 256, 256), 256)
            mid[:, lanes] = jnp.dot(tv[...], uv[:, lanes], preferred_element_type=F32).astype(BF)
            return 0
        lax.fori_loop(0, VIRT // 256, body, 0)

    def onebody():
        fcopy.wait()
        mask_virt(fv)
        def body(b, _):
            lanes = pl.ds(pl.multiple_of(b * 256, 256), 256)
            ob[:, lanes] = jnp.dot(tv[...], fv[:, lanes], preferred_element_type=F32)
            return 0
        lax.fori_loop(0, VIRT // 256, body, 0)

    def dots(c, groups, part=None):
        w = WIDTHS[c]
        size = ROWS // (2 if part is None else PARTS[c])

        def product(rows, h, start, count):
            ks = pl.ds(pl.multiple_of((h * SIDE + start) * SIDE * HALF, SIDE * HALF), count * SIDE * HALF)
            blocks = ts[c][pl.ds((h * SIDE + start) * SIDE, count * SIDE)].reshape(count * SIDE * HALF, w)
            return jnp.dot(xt[rows, ks], blocks, preferred_element_type=F32)

        def body(step, _):
            own = pl.ds(step * size, size)
            rows = pl.ds(pl.multiple_of(step * size * OCC_J, size * OCC_J), size * OCC_J)
            if groups == 0:
                total = jnp.dot(bd[rows, :], mid[:, STARTS[c]:STARTS[c] + w], preferred_element_type=F32)
            else:
                total = accs[c][own].reshape(size * OCC_J, w)
            for h in range(2):
                q, _ = axes(h)
                if groups < 2:
                    total = total + product(rows, h, (q // 2 if groups == 0 else 1 - q // 2) * 2, 2)
                else:
                    total = total + product(rows, h, 3 - q if groups == 2 else (q + 2) % SIDE, 1)
            accs[c][own] = total.reshape(size, SIDE, 2, COLS, w)
            return 0
        if part is None:
            lax.fori_loop(0, 2, body, 0)
        else:
            body(part, 0)

    def share(c, part):
        size = ROWS // PARTS[c]
        return pl.ds(part * size, size)

    def to_sibling(c, part):
        i = share(c, part)
        return pltpu.make_async_remote_copy(
            src_ref=s1s[c].at[i], dst_ref=r1s[c].at[i], send_sem=as_.at[4 * c + part], recv_sem=ar.at[4 * c + part],
            device_id=sibling, device_id_type=MESH)

    def SA(c, part=0):
        i = share(c, part)
        s1s[c][i] = accs[c][i, :, 1 - core].astype(BF)
        to_sibling(c, part).start()

    def SB(c, part=0):
        w, i = WIDTHS[c], share(c, part)
        cols = pl.ds(STARTS[c], w)
        to_sibling(c, part).wait_recv()
        for d in (2, 1, 3):
            to = (z + d) % SIDE
            s2s[c][d - 1, i] = (accs[c][i, to, core] + r1s[c][i, to].astype(F32)).astype(BF)
            pltpu.make_async_remote_copy(
                src_ref=s2s[c].at[d - 1, i], dst_ref=r2_hbm.at[d - 1, i, :, cols], send_sem=bs.at[0], recv_sem=br.at[0],
                device_id=zdev(d), device_id_type=MESH).start()
        size = ROWS // PARTS[c]
        one = ob[part * size * COLS:(part + 1) * size * COLS, STARTS[c]:STARTS[c] + w].reshape(size, COLS, w)
        finv[i, :, cols] = accs[c][i, z, core] + r1s[c][i, z].astype(F32) + one
        pltpu.make_async_copy(finv.at[i, :, cols], fin_hbm.at[i, :, cols], osem.at[0]).start()

    for name, *args in SCHEDULE:
        dict(D1=D1, O=O, E1=E1, N=N, E2=E2, G=G, H=H, prep=prep, build=build, middle=middle, onebody=onebody, dots=dots, SA=SA, SB=SB)[name](*args)

    for c in range(n):
        ref = ts[c].at[pl.ds(0, 30)]
        pltpu.make_async_remote_copy(
            src_ref=ref, dst_ref=ref, send_sem=gs.at[c], recv_sem=gr.at[c], device_id=sibling, device_id_type=MESH).wait_send()
        for part in range(PARTS[c]):
            to_sibling(c, part).wait_send()
    pltpu.make_async_copy(finv, fin_hbm, osem.at[0]).wait()
    last = pltpu.make_async_remote_copy(
        src_ref=r2_hbm, dst_ref=r2_hbm, send_sem=bs.at[0], recv_sem=br.at[0], device_id=sibling, device_id_type=MESH)
    last.wait_send()
    last.wait_recv()


def local(amplitudes, hole_int, ladder_int, cycle_virt, cycle_occ, irrep_rows, irrep_cols, irrep_virt):
    vm, dma = pltpu.VMEM, pltpu.SemaphoreType.DMA
    any_ = pl.BlockSpec(memory_space=pl.ANY)
    scratch = [
        vm((ROWS * COLS, VIRT), BF), vm((2, SIDE, ROWS, SIDE, HALF, OCC_J), BF), vm((ROWS * OCC_J, OCC_I * COLS), BF),
        vm((VIRT, VIRT), BF), vm((VIRT, VIRT), BF), vm((2, SIDE, SIDE, HALF, OCC_J), BF), vm((OCC_J, OCC_J), jnp.int32),
        vm((VIRT, 128), BF), vm((ROWS * OCC_J, ROWS * COLS), BF), vm((ROWS * COLS, VIRT), BF), vm((ROWS * COLS, VIRT), F32),
        vm((ROWS, COLS, VIRT), F32), vm((OCC_J, OCC_J), BF), vm((1, OCC_J), jnp.int32), vm((1, VIRT), jnp.int32),
        pltpu.SMEM((OCC_I,), jnp.int32),
    ]
    scratch += [vm((2 * SIDE * SIDE, HALF, w), BF) for w in WIDTHS]
    scratch += [vm((ROWS, SIDE, 2, COLS, w), F32) for w in WIDTHS]
    scratch += [vm((ROWS, SIDE, COLS, w), BF) for w in WIDTHS]
    scratch += [vm((ROWS, SIDE, COLS, w), BF) for w in WIDTHS]
    scratch += [vm((SIDE - 1, ROWS, COLS, w), BF) for w in WIDTHS]
    scratch += [dma((k,)) for k in (1, 1, 2, 2, 1, 4, NCH, NCH * EVENTS, 4 * NCH, 4 * NCH, 1, 1)]
    own, others = pl.pallas_call(
        kernel,
        out_shape=(jax.ShapeDtypeStruct((ROWS, COLS, VIRT), F32), jax.ShapeDtypeStruct((SIDE - 1, ROWS, COLS, VIRT), BF)),
        in_specs=[any_] * 8,
        out_specs=(any_, any_),
        scratch_shapes=scratch,
        compiler_params=pltpu.CompilerParams(collective_id=0, has_side_effects=True, vmem_limit_bytes=60 * 2**20),
        name="residual",
    )(amplitudes.reshape(ROWS * COLS, VIRT), hole_int.reshape(ROWS, SIDE, SIDE, 2, HALF, OCC_J), ladder_int, cycle_virt,
      cycle_occ, irrep_rows, irrep_cols.reshape(1, OCC_J), irrep_virt.reshape(1, VIRT))
    return (own + others[0].astype(F32) + others[1].astype(F32) + others[2].astype(F32)).astype(BF)


def solution(mesh):
    placed = (P("row", "col", None), P("row", None, "col", None), P(), P(), P(), P(), P(), P())
    return jax.shard_map(
        local, mesh=mesh, in_specs=placed, out_specs=P("row", "col", None), check_vma=False
    )
```

```python
import functools

import jax
import jax.numpy as jnp
from jax import lax
from jax.experimental import pallas as pl
from jax.experimental.pallas import tpu as pltpu
from jax.sharding import PartitionSpec as P

MESH = pl.DeviceIdType.MESH
BF, F32 = jnp.bfloat16, jnp.float32
SIDE = 4
ROWS, COLS, VIRT = 12, 16, 1024
OCC_I, OCC_J = 192, 128
HALF = ROWS * COLS // 2
WIDTHS = (256, 256, 256, 256)
STARTS = tuple(sum(WIDTHS[:c]) for c in range(len(WIDTHS)))
NCH = len(WIDTHS)
PARTS = (1, 1, 1, 4)
EVENTS = 8


SCHEDULE = (
    ('D1', 0), ('O', 0), ('D1', 1), ('D1', 2), ('load_rest',), ('prep',), ('build', True), ('E1', 0), ('D1', 3), ('N', 0), ('middle',), ('E1', 1), ('E2', 0), ('N', 1), ('build', False), ('O', 1), ('G', 0, 3), ('G', 0, 4), ('G', 0, 2), ('onebody',), ('G', 0, 5), ('E2', 1), ('E1', 2), ('dots', 0, 0), ('O', 2), ('G', 1, 2), ('N', 2), ('G', 1, 3), ('G', 1, 4), ('H', 0), ('dots', 0, 1), ('G', 1, 5), ('E2', 2), ('SA', 0), ('E1', 3), ('dots', 1, 0), ('N', 3), ('SB', 0), ('G', 2, 3), ('G', 2, 4), ('G', 2, 2), ('H', 1), ('dots', 1, 1), ('G', 2, 5), ('O', 3), ('SA', 1), ('E2', 3), ('dots', 2, 0), ('G', 3, 4), ('G', 3, 3), ('SB', 1), ('H', 2), ('dots', 2, 1), ('G', 3, 2), ('SA', 2), ('G', 3, 5), ('dots', 3, 0), ('SB', 2), ('dots', 3, 2), ('H', 3), ('dots', 3, 3, 0), ('SA', 3, 0), ('dots', 3, 3, 1), ('SA', 3, 1), ('dots', 3, 3, 2), ('SA', 3, 2), ('dots', 3, 3, 3), ('SA', 3, 3), ('SB', 3, 0), ('SB', 3, 1), ('SB', 3, 2), ('SB', 3, 3),
)


def kernel(t_hbm, x_hbm, f_hbm, u_hbm, z_hbm, rows_hbm, cols_hbm, virt_hbm, fin_hbm, r2_hbm,
           tv, xraw, xt, fv, uv, dk, cs, vcol, bd, mid, ob, finv, z_ref, cols_v, virt_v, rows_s, *rest):
    n = NCH
    ts, accs, s1s, r1s, s2s = (rest[i * n:(i + 1) * n] for i in range(5))
    (tsem, tvsem, xsem, fusem, osem, smsem, gs, gr, as_, ar, bs, br) = rest[5 * n:]
    row, col = lax.axis_index("row"), lax.axis_index("col")
    y, x = row // SIDE, row % SIDE
    z, core = col // 2, col % 2

    def axes(h):
        return (y, x) if h == 0 else (x, y)

    def dev(h, p, q):
        p, q = p % SIDE, q % SIDE
        return {"row": q * SIDE + p if h == 0 else p * SIDE + q, "col": col}

    def owner(h, g, m):
        return g * SIDE + m if h == 0 else m * SIDE + g

    zdev = lambda d: {"row": row, "col": (z + d) % SIDE * 2 + core}
    sibling = {"row": row, "col": col + 1 - 2 * core}

    small = []
    for i, (a, b) in enumerate(((rows_hbm, rows_s), (cols_hbm, cols_v), (z_hbm, z_ref), (virt_hbm, virt_v))):
        cp = pltpu.make_async_copy(a, b, smsem.at[i])
        small.append(cp)

    def block(h, g, m):
        return (h * SIDE + g) * SIDE + m

    bar = pltpu.get_barrier_semaphore()
    for h in range(2):
        q, p = axes(h)
        for d in (1, 3):
            pl.semaphore_signal(bar, inc=1, device_id=dev(h, p + d, q), device_id_type=MESH)
    pl.semaphore_signal(bar, inc=1, device_id=sibling, device_id_type=MESH)
    for d in (1, 2, 3):
        pl.semaphore_signal(bar, inc=1, device_id=zdev(d), device_id_type=MESH)

    tvcopy = pltpu.make_async_copy(t_hbm, tv, tvsem.at[0])
    ucopy = pltpu.make_async_copy(u_hbm, uv, fusem.at[1])
    fcopy = pltpu.make_async_copy(f_hbm, fv, fusem.at[0])

    def load():
        for c in range(n):
            for h in range(2):
                q, p = axes(h)
                pltpu.make_async_copy(
                    t_hbm.at[pl.ds(h * HALF, HALF), pl.ds(STARTS[c], WIDTHS[c])], ts[c].at[block(h, q, p)], tsem.at[0]).start()
        for cp in small:
            cp.start()
        tvcopy.start()

    def load_rest():
        for first in (True, False):
            for h in range(2):
                for o in range(2):
                    q, _ = axes(h)
                    g = (q // 2 if first else 1 - q // 2) * 2 + o
                    source = x_hbm.at[:, g, :, h] if h == 0 else x_hbm.at[:, :, g, h]
                    pltpu.make_async_copy(source, xraw.at[h, g], xsem.at[1 - first]).start()
            if first:
                ucopy.start()
        fcopy.start()

    load()
    pl.semaphore_wait(bar, 8)

    def send(c, h, kind, d, ref, source=None):
        q, p = axes(h)
        s = 1 if d == 0 else 3
        to = dev(h, p + s, q) if kind < 2 else dev(h, p, q + s)
        pltpu.make_async_remote_copy(
            src_ref=ref if source is None else source, dst_ref=ref, send_sem=gs.at[c],
            recv_sem=gr.at[c * EVENTS + kind], device_id=to,
            device_id_type=MESH).start()

    def arrived(c, kind, blocks):
        ref = ts[c].at[pl.ds(0, blocks)]
        pltpu.make_async_remote_copy(
            src_ref=ref, dst_ref=ref, send_sem=gs.at[c], recv_sem=gr.at[c * EVENTS + kind], device_id=sibling,
            device_id_type=MESH).wait_recv()

    OFF = {2: 0, 3: 3, 4: 1, 5: 2}
    FW = {0: (2, 4), 1: (3, 5)}

    def src(v, d):
        return (v + (3 if d == 0 else 1)) % SIDE

    def first_sends(c, kind):
        for h in range(2):
            q, p = axes(h)
            for d in range(2):
                send(c, h, kind, d, ts[c].at[block(h, q, p)],
                     t_hbm.at[pl.ds(h * HALF, HALF), pl.ds(STARTS[c], WIDTHS[c])])

    def D1(c):
        first_sends(c, 0)

    def O(c):
        first_sends(c, 2)

    def E1(c):
        arrived(c, 0, 4)
        for h in range(2):
            q, p = axes(h)
            for d in range(2):
                send(c, h, 1, d, ts[c].at[block(h, q, src(p, d)), pl.ds(HALF // 2 * d, HALF // 2)])

    def N(c):
        for k in range(2):
            for h in range(2):
                q, p = axes(h)
                for d in range(2):
                    kind = (4, 3)[k ^ d]
                    send(c, h, kind, d, ts[c].at[block(h, q, (p + OFF[kind]) % SIDE)])

    def E2(c):
        arrived(c, 1, 2)
        for h in range(2):
            q, p = axes(h)
            for d in range(2):
                send(c, h, 5, d, ts[c].at[block(h, q, (p + 2) % SIDE)])

    def G(c, *ks):
        for k in ks or (2, 3, 4, 5):
            arrived(c, k, 4)
            d = 0 if k in FW[0] else 1
            for h in range(2):
                q, p = axes(h)
                send(c, h, 6 + FW[d].index(k), d, ts[c].at[block(h, src(q, d), (p + OFF[k]) % SIDE)])

    def H(c):
        arrived(c, 6, 4)
        arrived(c, 7, 4)

    def prep():
        small[1].wait()
        small[0].wait()
        row_c = cols_v[...]
        cs[...] = jnp.broadcast_to(row_c, (OCC_J, OCC_J)).T
        base = cs[pl.ds(pl.multiple_of(col * COLS, COLS), COLS), :] ^ jnp.broadcast_to(row_c, (COLS, OCC_J))
        for h in range(2):
            def body(b, _, h=h):
                r = owner(h, b // SIDE, b % SIDE)
                for kk in range(ROWS // 2):
                    v = base ^ rows_s[r * ROWS + h * (ROWS // 2) + kk]
                    dk[h, b // SIDE, b % SIDE, kk * COLS:(kk + 1) * COLS, :] = v.astype(F32).astype(BF)
                return 0
            lax.fori_loop(0, SIDE * SIDE, body, 0)
        small[2].wait()
        lane = lax.broadcasted_iota(jnp.int32, (OCC_J, ROWS * COLS), 1)
        sub = lax.broadcasted_iota(jnp.int32, (OCC_J, ROWS * COLS), 0)
        pick = jnp.where(sub == col * COLS + (lane & (COLS - 1)), 1.0, 0.0).astype(BF)
        tiled = jnp.dot(z_ref[...], pick, preferred_element_type=F32)
        for i in range(ROWS):
            bd[i * OCC_J:(i + 1) * OCC_J, :] = jnp.where((lane >> 4) == i, tiled, 0.0).astype(BF)
        small[3].wait()
        tvcopy.wait()
        pltpu.make_async_copy(t_hbm, tv, tsem.at[0]).wait()
        for b in range(VIRT // 128):
            piece = virt_v[:, b * 128:(b + 1) * 128].astype(F32)
            vcol[b * 128:(b + 1) * 128, :] = jnp.broadcast_to(piece, (128, 128)).T.astype(BF)

    def build(first):
        pltpu.make_async_copy(xraw.at[0], xraw.at[0], xsem.at[1 - first]).wait()
        def body(b, _):
            h, o = b // 2, b % 2
            q = y + h * (x - y)
            pr = q // 2 if first else 1 - q // 2
            g = pr * 2 + o
            start = pl.multiple_of((h * SIDE + g) * SIDE * HALF, SIDE * HALF)
            for i in range(ROWS):
                xs = xraw[h, g, i].reshape(SIDE * HALF, OCC_J)
                keep = dk[h, g].reshape(SIDE * HALF, OCC_J) == rows_s[row * ROWS + i].astype(F32).astype(BF)
                xs = jnp.where(keep, xs, jnp.zeros((), BF))
                xt[i * OCC_J:(i + 1) * OCC_J, pl.ds(start, SIDE * HALF)] = xs.T
            return 0
        lax.fori_loop(0, 4, body, 0)

    def mask_virt(w):
        def body(b, _):
            rows = pl.ds(pl.multiple_of(b * 128, 128), 128)
            for j in range(VIRT // 128):
                lanes = slice(j * 128, (j + 1) * 128)
                keep = vcol[rows, :] == virt_v[:, lanes].astype(F32).astype(BF)
                w[rows, lanes] = jnp.where(keep, w[rows, lanes], jnp.zeros((), BF))
            return 0
        lax.fori_loop(0, VIRT // 128, body, 0)

    def middle():
        ucopy.wait()
        mask_virt(uv)
        def body(b, _):
            lanes = pl.ds(pl.multiple_of(b * 256, 256), 256)
            mid[:, lanes] = jnp.dot(tv[...], uv[:, lanes], preferred_element_type=F32).astype(BF)
            return 0
        lax.fori_loop(0, VIRT // 256, body, 0)

    def onebody():
        fcopy.wait()
        mask_virt(fv)
        def body(b, _):
            lanes = pl.ds(pl.multiple_of(b * 256, 256), 256)
            ob[:, lanes] = jnp.dot(tv[...], fv[:, lanes], preferred_element_type=F32)
            return 0
        lax.fori_loop(0, VIRT // 256, body, 0)

    def dots(c, groups, part=None):
        w = WIDTHS[c]
        size = ROWS // (2 if part is None else PARTS[c])

        def product(rows, h, start, count):
            ks = pl.ds(pl.multiple_of((h * SIDE + start) * SIDE * HALF, SIDE * HALF), count * SIDE * HALF)
            blocks = ts[c][pl.ds((h * SIDE + start) * SIDE, count * SIDE)].reshape(count * SIDE * HALF, w)
            return jnp.dot(xt[rows, ks], blocks, preferred_element_type=F32)

        def body(step, _):
            own = pl.ds(step * size, size)
            rows = pl.ds(pl.multiple_of(step * size * OCC_J, size * OCC_J), size * OCC_J)
            if groups == 0:
                total = jnp.dot(bd[rows, :], mid[:, STARTS[c]:STARTS[c] + w], preferred_element_type=F32)
            else:
                total = accs[c][own].reshape(size * OCC_J, w)
            for h in range(2):
                q, _ = axes(h)
                if groups < 2:
                    total = total + product(rows, h, (q // 2 if groups == 0 else 1 - q // 2) * 2, 2)
                else:
                    total = total + product(rows, h, 3 - q if groups == 2 else (q + 2) % SIDE, 1)
            accs[c][own] = total.reshape(size, SIDE, 2, COLS, w)
            return 0
        if part is None:
            lax.fori_loop(0, 2, body, 0)
        else:
            body(part, 0)

    def share(c, part):
        size = ROWS // PARTS[c]
        return pl.ds(part * size, size)

    def to_sibling(c, part):
        i = share(c, part)
        return pltpu.make_async_remote_copy(
            src_ref=s1s[c].at[i], dst_ref=r1s[c].at[i], send_sem=as_.at[4 * c + part], recv_sem=ar.at[4 * c + part],
            device_id=sibling, device_id_type=MESH)

    def SA(c, part=0):
        i = share(c, part)
        s1s[c][i] = accs[c][i, :, 1 - core].astype(BF)
        to_sibling(c, part).start()

    def SB(c, part=0):
        w, i = WIDTHS[c], share(c, part)
        cols = pl.ds(STARTS[c], w)
        to_sibling(c, part).wait_recv()
        for d in (2, 1, 3):
            to = (z + d) % SIDE
            s2s[c][d - 1, i] = (accs[c][i, to, core] + r1s[c][i, to].astype(F32)).astype(BF)
            pltpu.make_async_remote_copy(
                src_ref=s2s[c].at[d - 1, i], dst_ref=r2_hbm.at[d - 1, i, :, cols], send_sem=bs.at[0], recv_sem=br.at[0],
                device_id=zdev(d), device_id_type=MESH).start()
        size = ROWS // PARTS[c]
        one = ob[part * size * COLS:(part + 1) * size * COLS, STARTS[c]:STARTS[c] + w].reshape(size, COLS, w)
        finv[i, :, cols] = accs[c][i, z, core] + r1s[c][i, z].astype(F32) + one
        pltpu.make_async_copy(finv.at[i, :, cols], fin_hbm.at[i, :, cols], osem.at[0]).start()

    for name, *args in SCHEDULE:
        dict(load_rest=load_rest, D1=D1, O=O, E1=E1, N=N, E2=E2, G=G, H=H, prep=prep, build=build, middle=middle, onebody=onebody, dots=dots, SA=SA, SB=SB)[name](*args)

    for c in range(n):
        ref = ts[c].at[pl.ds(0, 30)]
        pltpu.make_async_remote_copy(
            src_ref=ref, dst_ref=ref, send_sem=gs.at[c], recv_sem=gr.at[c], device_id=sibling, device_id_type=MESH).wait_send()
        for part in range(PARTS[c]):
            to_sibling(c, part).wait_send()
    pltpu.make_async_copy(finv, fin_hbm, osem.at[0]).wait()
    last = pltpu.make_async_remote_copy(
        src_ref=r2_hbm, dst_ref=r2_hbm, send_sem=bs.at[0], recv_sem=br.at[0], device_id=sibling, device_id_type=MESH)
    last.wait_send()
    last.wait_recv()


def local(amplitudes, hole_int, ladder_int, cycle_virt, cycle_occ, irrep_rows, irrep_cols, irrep_virt):
    vm, dma = pltpu.VMEM, pltpu.SemaphoreType.DMA
    any_ = pl.BlockSpec(memory_space=pl.ANY)
    scratch = [
        vm((ROWS * COLS, VIRT), BF), vm((2, SIDE, ROWS, SIDE, HALF, OCC_J), BF), vm((ROWS * OCC_J, OCC_I * COLS), BF),
        vm((VIRT, VIRT), BF), vm((VIRT, VIRT), BF), vm((2, SIDE, SIDE, HALF, OCC_J), BF), vm((OCC_J, OCC_J), jnp.int32),
        vm((VIRT, 128), BF), vm((ROWS * OCC_J, ROWS * COLS), BF), vm((ROWS * COLS, VIRT), BF), vm((ROWS * COLS, VIRT), F32),
        vm((ROWS, COLS, VIRT), F32), vm((OCC_J, OCC_J), BF), vm((1, OCC_J), jnp.int32), vm((1, VIRT), jnp.int32),
        pltpu.SMEM((OCC_I,), jnp.int32),
    ]
    scratch += [vm((2 * SIDE * SIDE, HALF, w), BF) for w in WIDTHS]
    scratch += [vm((ROWS, SIDE, 2, COLS, w), F32) for w in WIDTHS]
    scratch += [vm((ROWS, SIDE, COLS, w), BF) for w in WIDTHS]
    scratch += [vm((ROWS, SIDE, COLS, w), BF) for w in WIDTHS]
    scratch += [vm((SIDE - 1, ROWS, COLS, w), BF) for w in WIDTHS]
    scratch += [dma((k,)) for k in (1, 1, 2, 2, 1, 4, NCH, NCH * EVENTS, 4 * NCH, 4 * NCH, 1, 1)]
    own, others = pl.pallas_call(
        kernel,
        out_shape=(jax.ShapeDtypeStruct((ROWS, COLS, VIRT), F32), jax.ShapeDtypeStruct((SIDE - 1, ROWS, COLS, VIRT), BF)),
        in_specs=[any_] * 8,
        out_specs=(any_, any_),
        scratch_shapes=scratch,
        compiler_params=pltpu.CompilerParams(collective_id=0, has_side_effects=True, vmem_limit_bytes=60 * 2**20),
        name="residual",
    )(amplitudes.reshape(ROWS * COLS, VIRT), hole_int.reshape(ROWS, SIDE, SIDE, 2, HALF, OCC_J), ladder_int, cycle_virt,
      cycle_occ, irrep_rows, irrep_cols.reshape(1, OCC_J), irrep_virt.reshape(1, VIRT))
    return (own + others[0].astype(F32) + others[1].astype(F32) + others[2].astype(F32)).astype(BF)


def solution(mesh):
    placed = (P("row", "col", None), P("row", None, "col", None), P(), P(), P(), P(), P(), P())
    return jax.shard_map(
        local, mesh=mesh, in_specs=placed, out_specs=P("row", "col", None), check_vma=False
    )
```

```python
import functools

import jax
import jax.numpy as jnp
from jax import lax
from jax.experimental import pallas as pl
from jax.experimental.pallas import tpu as pltpu
from jax.sharding import PartitionSpec as P

MESH = pl.DeviceIdType.MESH
BF, F32 = jnp.bfloat16, jnp.float32
SIDE = 4
ROWS, COLS, VIRT = 12, 16, 1024
OCC_I, OCC_J = 192, 128
HALF = ROWS * COLS // 2
WIDTHS = (256, 256, 256, 256)
STARTS = tuple(sum(WIDTHS[:c]) for c in range(len(WIDTHS)))
NCH = len(WIDTHS)
PARTS = (1, 1, 1, 4)
EVENTS = 8


SCHEDULE = (
    ('D1', 0), ('O', 0), ('D1', 1), ('D1', 2), ('load_rest',), ('prep',), ('build', True), ('E1', 0), ('D1', 3), ('N', 0), ('middle',), ('E1', 1), ('E2', 0), ('N', 1), ('build', False), ('O', 1), ('G', 0, 3), ('G', 0, 4), ('G', 0, 2), ('onebody',), ('G', 0, 5), ('E2', 1), ('E1', 2), ('dots', 0, 0), ('O', 2), ('G', 1, 2), ('N', 2), ('G', 1, 3), ('G', 1, 4), ('H', 0), ('dots', 0, 1), ('G', 1, 5), ('E2', 2), ('SA', 0), ('E1', 3), ('dots', 1, 0), ('N', 3), ('SB', 0), ('G', 2, 3), ('G', 2, 4), ('G', 2, 2), ('H', 1), ('dots', 1, 1), ('G', 2, 5), ('O', 3), ('SA', 1), ('E2', 3), ('dots', 2, 0), ('G', 3, 4), ('G', 3, 3), ('SB', 1), ('H', 2), ('dots', 2, 1), ('G', 3, 2), ('SA', 2), ('G', 3, 5), ('dots', 3, 0), ('SB', 2), ('dots', 3, 2), ('H', 3), ('dots', 3, 3, 0), ('SA', 3, 0), ('dots', 3, 3, 1), ('SA', 3, 1), ('dots', 3, 3, 2), ('SA', 3, 2), ('dots', 3, 3, 3), ('SA', 3, 3), ('SB', 3, 0), ('SB', 3, 1), ('SB', 3, 2), ('SB', 3, 3),
)


def kernel(t_hbm, x_hbm, f_hbm, u_hbm, z_hbm, rows_hbm, cols_hbm, virt_hbm, fin_hbm, r2_hbm,
           tv, xraw, xt, fv, uv, dk, cs, vcol, bd, mid, ob, finv, z_ref, cols_v, virt_v, rows_s, *rest):
    n = NCH
    ts, accs, s1s, r1s, s2s = (rest[i * n:(i + 1) * n] for i in range(5))
    (tsem, tvsem, xsem, fusem, osem, smsem, gs, gr, as_, ar, bs, br) = rest[5 * n:]
    row, col = lax.axis_index("row"), lax.axis_index("col")
    y, x = row // SIDE, row % SIDE
    z, core = col // 2, col % 2

    def axes(h):
        return (y, x) if h == 0 else (x, y)

    def dev(h, p, q):
        p, q = p % SIDE, q % SIDE
        return {"row": q * SIDE + p if h == 0 else p * SIDE + q, "col": col}

    def owner(h, g, m):
        return g * SIDE + m if h == 0 else m * SIDE + g

    zdev = lambda d: {"row": row, "col": (z + d) % SIDE * 2 + core}
    sibling = {"row": row, "col": col + 1 - 2 * core}

    small = []
    for i, (a, b) in enumerate(((rows_hbm, rows_s), (cols_hbm, cols_v), (z_hbm, z_ref), (virt_hbm, virt_v))):
        cp = pltpu.make_async_copy(a, b, smsem.at[i])
        small.append(cp)

    def block(h, g, m):
        return (h * SIDE + g) * SIDE + m

    bar = pltpu.get_barrier_semaphore()
    for h in range(2):
        q, p = axes(h)
        for d in (1, 3):
            pl.semaphore_signal(bar, inc=1, device_id=dev(h, p + d, q), device_id_type=MESH)
    pl.semaphore_signal(bar, inc=1, device_id=sibling, device_id_type=MESH)
    for d in (1, 2, 3):
        pl.semaphore_signal(bar, inc=1, device_id=zdev(d), device_id_type=MESH)

    tvcopy = pltpu.make_async_copy(t_hbm, tv, tvsem.at[0])
    ucopy = pltpu.make_async_copy(u_hbm, uv, fusem.at[1])
    fcopy = pltpu.make_async_copy(f_hbm, fv, fusem.at[0])

    def load():
        for c in range(n):
            for h in range(2):
                q, p = axes(h)
                pltpu.make_async_copy(
                    t_hbm.at[pl.ds(h * HALF, HALF), pl.ds(STARTS[c], WIDTHS[c])], ts[c].at[block(h, q, p)], tsem.at[0]).start()
        for cp in small:
            cp.start()
        tvcopy.start()

    def load_rest():
        for first in (True, False):
            for h in range(2):
                for o in range(2):
                    q, _ = axes(h)
                    g = (q // 2 if first else 1 - q // 2) * 2 + o
                    source = x_hbm.at[:, g, :, h] if h == 0 else x_hbm.at[:, :, g, h]
                    pltpu.make_async_copy(source, xraw.at[h, g], xsem.at[1 - first]).start()
            if first:
                ucopy.start()
        fcopy.start()

    load()
    pl.semaphore_wait(bar, 8)

    def send(c, h, kind, d, ref, source=None):
        q, p = axes(h)
        s = 1 if d == 0 else 3
        to = dev(h, p + s, q) if kind < 2 else dev(h, p, q + s)
        pltpu.make_async_remote_copy(
            src_ref=ref if source is None else source, dst_ref=ref, send_sem=gs.at[c],
            recv_sem=gr.at[c * EVENTS + kind], device_id=to,
            device_id_type=MESH).start()

    def arrived(c, kind, blocks):
        ref = ts[c].at[pl.ds(0, blocks)]
        pltpu.make_async_remote_copy(
            src_ref=ref, dst_ref=ref, send_sem=gs.at[c], recv_sem=gr.at[c * EVENTS + kind], device_id=sibling,
            device_id_type=MESH).wait_recv()

    OFF = {2: 0, 3: 3, 4: 1, 5: 2}
    FW = {0: (2, 4), 1: (3, 5)}

    def src(v, d):
        return (v + (3 if d == 0 else 1)) % SIDE

    def first_sends(c, kind):
        for h in range(2):
            q, p = axes(h)
            for d in range(2):
                send(c, h, kind, d, ts[c].at[block(h, q, p)],
                     t_hbm.at[pl.ds(h * HALF, HALF), pl.ds(STARTS[c], WIDTHS[c])])

    def D1(c):
        first_sends(c, 0)

    def O(c):
        first_sends(c, 2)

    def E1(c):
        arrived(c, 0, 4)
        for h in range(2):
            q, p = axes(h)
            for d in range(2):
                send(c, h, 1, d, ts[c].at[block(h, q, src(p, d)), pl.ds(HALF // 2 * d, HALF // 2)])

    def N(c):
        for k in range(2):
            for h in range(2):
                q, p = axes(h)
                for d in range(2):
                    kind = (4, 3)[k ^ d]
                    send(c, h, kind, d, ts[c].at[block(h, q, (p + OFF[kind]) % SIDE)])

    def E2(c):
        arrived(c, 1, 2)
        for h in range(2):
            q, p = axes(h)
            for d in range(2):
                send(c, h, 5, d, ts[c].at[block(h, q, (p + 2) % SIDE)])

    def G(c, *ks):
        for k in ks or (2, 3, 4, 5):
            arrived(c, k, 4)
            d = 0 if k in FW[0] else 1
            for h in range(2):
                q, p = axes(h)
                send(c, h, 6 + FW[d].index(k), d, ts[c].at[block(h, src(q, d), (p + OFF[k]) % SIDE)])

    def H(c):
        arrived(c, 6, 4)
        arrived(c, 7, 4)

    def prep():
        small[1].wait()
        small[0].wait()
        row_c = cols_v[...]
        cs[...] = jnp.broadcast_to(row_c, (OCC_J, OCC_J)).T
        base = cs[pl.ds(pl.multiple_of(col * COLS, COLS), COLS), :] ^ jnp.broadcast_to(row_c, (COLS, OCC_J))
        for h in range(2):
            def body(b, _, h=h):
                r = owner(h, b // SIDE, b % SIDE)
                for kk in range(ROWS // 2):
                    v = base ^ rows_s[r * ROWS + h * (ROWS // 2) + kk]
                    dk[h, b // SIDE, b % SIDE, kk * COLS:(kk + 1) * COLS, :] = v.astype(F32).astype(BF)
                return 0
            lax.fori_loop(0, SIDE * SIDE, body, 0)
        small[2].wait()
        lane = lax.broadcasted_iota(jnp.int32, (OCC_J, ROWS * COLS), 1)
        sub = lax.broadcasted_iota(jnp.int32, (OCC_J, ROWS * COLS), 0)
        pick = jnp.where(sub == col * COLS + (lane & (COLS - 1)), 1.0, 0.0).astype(BF)
        tiled = jnp.dot(z_ref[...], pick, preferred_element_type=F32)
        for i in range(ROWS):
            bd[i * OCC_J:(i + 1) * OCC_J, :] = jnp.where((lane >> 4) == i, tiled, 0.0).astype(BF)
        small[3].wait()
        tvcopy.wait()
        pltpu.make_async_copy(t_hbm, tv, tsem.at[0]).wait()
        for b in range(VIRT // 128):
            piece = virt_v[:, b * 128:(b + 1) * 128].astype(F32)
            vcol[b * 128:(b + 1) * 128, :] = jnp.broadcast_to(piece, (128, 128)).T.astype(BF)

    def build(first):
        pltpu.make_async_copy(xraw.at[0], xraw.at[0], xsem.at[1 - first]).wait()
        def body(b, _):
            h, o = b // 2, b % 2
            q = y + h * (x - y)
            pr = q // 2 if first else 1 - q // 2
            g = pr * 2 + o
            start = pl.multiple_of((h * SIDE + g) * SIDE * HALF, SIDE * HALF)
            for i in range(ROWS):
                xs = xraw[h, g, i].reshape(SIDE * HALF, OCC_J)
                keep = dk[h, g].reshape(SIDE * HALF, OCC_J) == rows_s[row * ROWS + i].astype(F32).astype(BF)
                xs = jnp.where(keep, xs, jnp.zeros((), BF))
                xt[i * OCC_J:(i + 1) * OCC_J, pl.ds(start, SIDE * HALF)] = xs.T
            return 0
        lax.fori_loop(0, 4, body, 0)

    def mask_virt(w):
        def body(b, _):
            rows = pl.ds(pl.multiple_of(b * 128, 128), 128)
            for j in range(VIRT // 128):
                lanes = slice(j * 128, (j + 1) * 128)
                keep = vcol[rows, :] == virt_v[:, lanes].astype(F32).astype(BF)
                w[rows, lanes] = jnp.where(keep, w[rows, lanes], jnp.zeros((), BF))
            return 0
        lax.fori_loop(0, VIRT // 128, body, 0)

    def middle():
        ucopy.wait()
        mask_virt(uv)
        def body(b, _):
            lanes = pl.ds(pl.multiple_of(b * 256, 256), 256)
            mid[:, lanes] = jnp.dot(tv[...], uv[:, lanes], preferred_element_type=F32).astype(BF)
            return 0
        lax.fori_loop(0, VIRT // 256, body, 0)

    def onebody():
        fcopy.wait()
        mask_virt(fv)
        def body(b, _):
            lanes = pl.ds(pl.multiple_of(b * 256, 256), 256)
            ob[:, lanes] = jnp.dot(tv[...], fv[:, lanes], preferred_element_type=F32)
            return 0
        lax.fori_loop(0, VIRT // 256, body, 0)

    def dots(c, groups, part=None):
        w = WIDTHS[c]
        size = ROWS // (2 if part is None else PARTS[c])

        def product(rows, h, start, count):
            ks = pl.ds(pl.multiple_of((h * SIDE + start) * SIDE * HALF, SIDE * HALF), count * SIDE * HALF)
            blocks = ts[c][pl.ds((h * SIDE + start) * SIDE, count * SIDE)].reshape(count * SIDE * HALF, w)
            return jnp.dot(xt[rows, ks], blocks, preferred_element_type=F32)

        def body(step, _):
            own = pl.ds(step * size, size)
            rows = pl.ds(pl.multiple_of(step * size * OCC_J, size * OCC_J), size * OCC_J)
            if groups == 0:
                total = jnp.dot(bd[rows, :], mid[:, STARTS[c]:STARTS[c] + w], preferred_element_type=F32)
            else:
                total = accs[c][own].reshape(size * OCC_J, w)
            for h in range(2):
                q, _ = axes(h)
                if groups < 2:
                    total = total + product(rows, h, (q // 2 if groups == 0 else 1 - q // 2) * 2, 2)
                else:
                    total = total + product(rows, h, 3 - q if groups == 2 else (q + 2) % SIDE, 1)
            accs[c][own] = total.reshape(size, SIDE, 2, COLS, w)
            return 0
        if part is None:
            lax.fori_loop(0, 2, body, 0)
        else:
            body(part, 0)

    def share(c, part):
        size = ROWS // PARTS[c]
        return pl.ds(part * size, size)

    def to_sibling(c, part):
        i = share(c, part)
        return pltpu.make_async_remote_copy(
            src_ref=s1s[c].at[i], dst_ref=r1s[c].at[i], send_sem=as_.at[0], recv_sem=ar.at[c + part],
            device_id=sibling, device_id_type=MESH)

    def SA(c, part=0):
        i = share(c, part)
        s1s[c][i] = accs[c][i, :, 1 - core].astype(BF)
        to_sibling(c, part).start()

    def SB(c, part=0):
        w, i = WIDTHS[c], share(c, part)
        cols = pl.ds(STARTS[c], w)
        to_sibling(c, part).wait_recv()
        for d in (2, 1, 3):
            to = (z + d) % SIDE
            s2s[c][d - 1, i] = (accs[c][i, to, core] + r1s[c][i, to].astype(F32)).astype(BF)
            pltpu.make_async_remote_copy(
                src_ref=s2s[c].at[d - 1, i], dst_ref=r2_hbm.at[d - 1, i, :, cols], send_sem=bs.at[0], recv_sem=br.at[0],
                device_id=zdev(d), device_id_type=MESH).start()
        size = ROWS // PARTS[c]
        one = ob[part * size * COLS:(part + 1) * size * COLS, STARTS[c]:STARTS[c] + w].reshape(size, COLS, w)
        finv[i, :, cols] = accs[c][i, z, core] + r1s[c][i, z].astype(F32) + one
        pltpu.make_async_copy(finv.at[i, :, cols], fin_hbm.at[i, :, cols], osem.at[0]).start()

    for name, *args in SCHEDULE:
        dict(load_rest=load_rest, D1=D1, O=O, E1=E1, N=N, E2=E2, G=G, H=H, prep=prep, build=build, middle=middle, onebody=onebody, dots=dots, SA=SA, SB=SB)[name](*args)

    for c in range(n):
        ref = ts[c].at[pl.ds(0, 30)]
        pltpu.make_async_remote_copy(
            src_ref=ref, dst_ref=ref, send_sem=gs.at[c], recv_sem=gr.at[c], device_id=sibling, device_id_type=MESH).wait_send()
    pltpu.make_async_remote_copy(
        src_ref=ts[0], dst_ref=ts[0], send_sem=as_.at[0], recv_sem=ar.at[0], device_id=sibling, device_id_type=MESH).wait_send()
    pltpu.make_async_copy(finv, fin_hbm, osem.at[0]).wait()
    last = pltpu.make_async_remote_copy(
        src_ref=r2_hbm, dst_ref=r2_hbm, send_sem=bs.at[0], recv_sem=br.at[0], device_id=sibling, device_id_type=MESH)
    last.wait_send()
    last.wait_recv()


def local(amplitudes, hole_int, ladder_int, cycle_virt, cycle_occ, irrep_rows, irrep_cols, irrep_virt):
    vm, dma = pltpu.VMEM, pltpu.SemaphoreType.DMA
    any_ = pl.BlockSpec(memory_space=pl.ANY)
    scratch = [
        vm((ROWS * COLS, VIRT), BF), vm((2, SIDE, ROWS, SIDE, HALF, OCC_J), BF), vm((ROWS * OCC_J, OCC_I * COLS), BF),
        vm((VIRT, VIRT), BF), vm((VIRT, VIRT), BF), vm((2, SIDE, SIDE, HALF, OCC_J), BF), vm((OCC_J, OCC_J), jnp.int32),
        vm((VIRT, 128), BF), vm((ROWS * OCC_J, ROWS * COLS), BF), vm((ROWS * COLS, VIRT), BF), vm((ROWS * COLS, VIRT), F32),
        vm((ROWS, COLS, VIRT), F32), vm((OCC_J, OCC_J), BF), vm((1, OCC_J), jnp.int32), vm((1, VIRT), jnp.int32),
        pltpu.SMEM((OCC_I,), jnp.int32),
    ]
    scratch += [vm((2 * SIDE * SIDE, HALF, w), BF) for w in WIDTHS]
    scratch += [vm((ROWS, SIDE, 2, COLS, w), F32) for w in WIDTHS]
    scratch += [vm((ROWS, SIDE, COLS, w), BF) for w in WIDTHS]
    scratch += [vm((ROWS, SIDE, COLS, w), BF) for w in WIDTHS]
    scratch += [vm((SIDE - 1, ROWS, COLS, w), BF) for w in WIDTHS]
    scratch += [dma((k,)) for k in (1, 1, 2, 2, 1, 4, NCH, NCH * EVENTS, 1, NCH + PARTS[-1], 1, 1)]
    own, others = pl.pallas_call(
        kernel,
        out_shape=(jax.ShapeDtypeStruct((ROWS, COLS, VIRT), F32), jax.ShapeDtypeStruct((SIDE - 1, ROWS, COLS, VIRT), BF)),
        in_specs=[any_] * 8,
        out_specs=(any_, any_),
        scratch_shapes=scratch,
        compiler_params=pltpu.CompilerParams(collective_id=0, has_side_effects=True, vmem_limit_bytes=60 * 2**20),
        name="residual",
    )(amplitudes.reshape(ROWS * COLS, VIRT), hole_int.reshape(ROWS, SIDE, SIDE, 2, HALF, OCC_J), ladder_int, cycle_virt,
      cycle_occ, irrep_rows, irrep_cols.reshape(1, OCC_J), irrep_virt.reshape(1, VIRT))
    return (own + others[0].astype(F32) + others[1].astype(F32) + others[2].astype(F32)).astype(BF)


def solution(mesh):
    placed = (P("row", "col", None), P("row", None, "col", None), P(), P(), P(), P(), P(), P())
    return jax.shard_map(
        local, mesh=mesh, in_specs=placed, out_specs=P("row", "col", None), check_vma=False
    )
```

```python
import functools

import jax
import jax.numpy as jnp
from jax import lax
from jax.experimental import pallas as pl
from jax.experimental.pallas import tpu as pltpu
from jax.sharding import PartitionSpec as P

MESH = pl.DeviceIdType.MESH
BF, F32 = jnp.bfloat16, jnp.float32
SIDE = 4
ROWS, COLS, VIRT = 12, 16, 1024
OCC_I, OCC_J = 192, 128
HALF = ROWS * COLS // 2
WIDTHS = (256, 256, 256, 256)
STARTS = tuple(sum(WIDTHS[:c]) for c in range(len(WIDTHS)))
NCH = len(WIDTHS)
PARTS = (1, 1, 1, 6)
EVENTS = 8


SCHEDULE = (
    ('D1', 0), ('O', 0), ('D1', 1), ('D1', 2), ('load_rest',), ('prep',), ('build', True), ('E1', 0), ('D1', 3), ('N', 0), ('middle',), ('E1', 1), ('E2', 0), ('N', 1), ('build', False), ('O', 1), ('G', 0, 3), ('G', 0, 4), ('G', 0, 2), ('onebody',), ('G', 0, 5), ('E2', 1), ('E1', 2), ('dots', 0, 0), ('O', 2), ('G', 1, 2), ('N', 2), ('G', 1, 3), ('G', 1, 4), ('H', 0), ('dots', 0, 1), ('G', 1, 5), ('E2', 2), ('SA', 0), ('E1', 3), ('dots', 1, 0), ('N', 3), ('SB', 0), ('G', 2, 3), ('G', 2, 4), ('G', 2, 2), ('H', 1), ('dots', 1, 1), ('G', 2, 5), ('O', 3), ('SA', 1), ('E2', 3), ('dots', 2, 0), ('G', 3, 4), ('G', 3, 3), ('SB', 1), ('H', 2), ('dots', 2, 1), ('G', 3, 2), ('SA', 2), ('G', 3, 5), ('dots', 3, 0), ('SB', 2), ('dots', 3, 2), ('H', 3), ('dots', 3, 3, 0), ('SA', 3, 0), ('dots', 3, 3, 1), ('SA', 3, 1), ('dots', 3, 3, 2), ('SA', 3, 2), ('dots', 3, 3, 3), ('SA', 3, 3), ('SB', 3, 0), ('dots', 3, 3, 4), ('SA', 3, 4), ('SB', 3, 1), ('dots', 3, 3, 5), ('SA', 3, 5), ('SB', 3, 2), ('SB', 3, 3), ('SB', 3, 4), ('SB', 3, 5),
)


def kernel(t_hbm, x_hbm, f_hbm, u_hbm, z_hbm, rows_hbm, cols_hbm, virt_hbm, fin_hbm, r2_hbm,
           tv, xraw, xt, fv, uv, dk, cs, vcol, bd, mid, ob, finv, z_ref, cols_v, virt_v, rows_s, *rest):
    n = NCH
    ts, accs, s1s, r1s, s2s = (rest[i * n:(i + 1) * n] for i in range(5))
    (tsem, tvsem, xsem, fusem, osem, smsem, gs, gr, as_, ar, bs, br) = rest[5 * n:]
    row, col = lax.axis_index("row"), lax.axis_index("col")
    y, x = row // SIDE, row % SIDE
    z, core = col // 2, col % 2

    def axes(h):
        return (y, x) if h == 0 else (x, y)

    def dev(h, p, q):
        p, q = p % SIDE, q % SIDE
        return {"row": q * SIDE + p if h == 0 else p * SIDE + q, "col": col}

    def owner(h, g, m):
        return g * SIDE + m if h == 0 else m * SIDE + g

    zdev = lambda d: {"row": row, "col": (z + d) % SIDE * 2 + core}
    sibling = {"row": row, "col": col + 1 - 2 * core}

    small = []
    for i, (a, b) in enumerate(((rows_hbm, rows_s), (cols_hbm, cols_v), (z_hbm, z_ref), (virt_hbm, virt_v))):
        cp = pltpu.make_async_copy(a, b, smsem.at[i])
        small.append(cp)

    def block(h, g, m):
        return (h * SIDE + g) * SIDE + m

    bar = pltpu.get_barrier_semaphore()
    for h in range(2):
        q, p = axes(h)
        for d in (1, 3):
            pl.semaphore_signal(bar, inc=1, device_id=dev(h, p + d, q), device_id_type=MESH)
    pl.semaphore_signal(bar, inc=1, device_id=sibling, device_id_type=MESH)
    for d in (1, 2, 3):
        pl.semaphore_signal(bar, inc=1, device_id=zdev(d), device_id_type=MESH)

    tvcopy = pltpu.make_async_copy(t_hbm, tv, tvsem.at[0])
    ucopy = pltpu.make_async_copy(u_hbm, uv, fusem.at[1])
    fcopy = pltpu.make_async_copy(f_hbm, fv, fusem.at[0])

    def load():
        for c in range(n):
            for h in range(2):
                q, p = axes(h)
                pltpu.make_async_copy(
                    t_hbm.at[pl.ds(h * HALF, HALF), pl.ds(STARTS[c], WIDTHS[c])], ts[c].at[block(h, q, p)], tsem.at[0]).start()
        for cp in small:
            cp.start()
        tvcopy.start()

    def load_rest():
        for first in (True, False):
            for h in range(2):
                for o in range(2):
                    q, _ = axes(h)
                    g = (q // 2 if first else 1 - q // 2) * 2 + o
                    source = x_hbm.at[:, g, :, h] if h == 0 else x_hbm.at[:, :, g, h]
                    pltpu.make_async_copy(source, xraw.at[h, g], xsem.at[1 - first]).start()
            if first:
                ucopy.start()
        fcopy.start()

    load()
    pl.semaphore_wait(bar, 8)

    def send(c, h, kind, d, ref, source=None):
        q, p = axes(h)
        s = 1 if d == 0 else 3
        to = dev(h, p + s, q) if kind < 2 else dev(h, p, q + s)
        pltpu.make_async_remote_copy(
            src_ref=ref if source is None else source, dst_ref=ref, send_sem=gs.at[c],
            recv_sem=gr.at[c * EVENTS + kind], device_id=to,
            device_id_type=MESH).start()

    def arrived(c, kind, blocks):
        ref = ts[c].at[pl.ds(0, blocks)]
        pltpu.make_async_remote_copy(
            src_ref=ref, dst_ref=ref, send_sem=gs.at[c], recv_sem=gr.at[c * EVENTS + kind], device_id=sibling,
            device_id_type=MESH).wait_recv()

    OFF = {2: 0, 3: 3, 4: 1, 5: 2}
    FW = {0: (2, 4), 1: (3, 5)}

    def src(v, d):
        return (v + (3 if d == 0 else 1)) % SIDE

    def first_sends(c, kind):
        for h in range(2):
            q, p = axes(h)
            for d in range(2):
                send(c, h, kind, d, ts[c].at[block(h, q, p)],
                     t_hbm.at[pl.ds(h * HALF, HALF), pl.ds(STARTS[c], WIDTHS[c])])

    def D1(c):
        first_sends(c, 0)

    def O(c):
        first_sends(c, 2)

    def E1(c):
        arrived(c, 0, 4)
        for h in range(2):
            q, p = axes(h)
            for d in range(2):
                send(c, h, 1, d, ts[c].at[block(h, q, src(p, d)), pl.ds(HALF // 2 * d, HALF // 2)])

    def N(c):
        for k in range(2):
            for h in range(2):
                q, p = axes(h)
                for d in range(2):
                    kind = (4, 3)[k ^ d]
                    send(c, h, kind, d, ts[c].at[block(h, q, (p + OFF[kind]) % SIDE)])

    def E2(c):
        arrived(c, 1, 2)
        for h in range(2):
            q, p = axes(h)
            for d in range(2):
                send(c, h, 5, d, ts[c].at[block(h, q, (p + 2) % SIDE)])

    def G(c, *ks):
        for k in ks or (2, 3, 4, 5):
            arrived(c, k, 4)
            d = 0 if k in FW[0] else 1
            for h in range(2):
                q, p = axes(h)
                send(c, h, 6 + FW[d].index(k), d, ts[c].at[block(h, src(q, d), (p + OFF[k]) % SIDE)])

    def H(c):
        arrived(c, 6, 4)
        arrived(c, 7, 4)

    def prep():
        small[1].wait()
        small[0].wait()
        row_c = cols_v[...]
        cs[...] = jnp.broadcast_to(row_c, (OCC_J, OCC_J)).T
        base = cs[pl.ds(pl.multiple_of(col * COLS, COLS), COLS), :] ^ jnp.broadcast_to(row_c, (COLS, OCC_J))
        for h in range(2):
            def body(b, _, h=h):
                r = owner(h, b // SIDE, b % SIDE)
                for kk in range(ROWS // 2):
                    v = base ^ rows_s[r * ROWS + h * (ROWS // 2) + kk]
                    dk[h, b // SIDE, b % SIDE, kk * COLS:(kk + 1) * COLS, :] = v.astype(F32).astype(BF)
                return 0
            lax.fori_loop(0, SIDE * SIDE, body, 0)
        small[2].wait()
        lane = lax.broadcasted_iota(jnp.int32, (OCC_J, ROWS * COLS), 1)
        sub = lax.broadcasted_iota(jnp.int32, (OCC_J, ROWS * COLS), 0)
        pick = jnp.where(sub == col * COLS + (lane & (COLS - 1)), 1.0, 0.0).astype(BF)
        tiled = jnp.dot(z_ref[...], pick, preferred_element_type=F32)
        for i in range(ROWS):
            bd[i * OCC_J:(i + 1) * OCC_J, :] = jnp.where((lane >> 4) == i, tiled, 0.0).astype(BF)
        small[3].wait()
        tvcopy.wait()
        pltpu.make_async_copy(t_hbm, tv, tsem.at[0]).wait()
        for b in range(VIRT // 128):
            piece = virt_v[:, b * 128:(b + 1) * 128].astype(F32)
            vcol[b * 128:(b + 1) * 128, :] = jnp.broadcast_to(piece, (128, 128)).T.astype(BF)

    def build(first):
        pltpu.make_async_copy(xraw.at[0], xraw.at[0], xsem.at[1 - first]).wait()
        def body(b, _):
            h, o = b // 2, b % 2
            q = y + h * (x - y)
            pr = q // 2 if first else 1 - q // 2
            g = pr * 2 + o
            start = pl.multiple_of((h * SIDE + g) * SIDE * HALF, SIDE * HALF)
            for i in range(ROWS):
                xs = xraw[h, g, i].reshape(SIDE * HALF, OCC_J)
                keep = dk[h, g].reshape(SIDE * HALF, OCC_J) == rows_s[row * ROWS + i].astype(F32).astype(BF)
                xs = jnp.where(keep, xs, jnp.zeros((), BF))
                xt[i * OCC_J:(i + 1) * OCC_J, pl.ds(start, SIDE * HALF)] = xs.T
            return 0
        lax.fori_loop(0, 4, body, 0)

    def mask_virt(w):
        def body(b, _):
            rows = pl.ds(pl.multiple_of(b * 128, 128), 128)
            for j in range(VIRT // 128):
                lanes = slice(j * 128, (j + 1) * 128)
                keep = vcol[rows, :] == virt_v[:, lanes].astype(F32).astype(BF)
                w[rows, lanes] = jnp.where(keep, w[rows, lanes], jnp.zeros((), BF))
            return 0
        lax.fori_loop(0, VIRT // 128, body, 0)

    def middle():
        ucopy.wait()
        mask_virt(uv)
        def body(b, _):
            lanes = pl.ds(pl.multiple_of(b * 256, 256), 256)
            mid[:, lanes] = jnp.dot(tv[...], uv[:, lanes], preferred_element_type=F32).astype(BF)
            return 0
        lax.fori_loop(0, VIRT // 256, body, 0)

    def onebody():
        fcopy.wait()
        mask_virt(fv)
        def body(b, _):
            lanes = pl.ds(pl.multiple_of(b * 256, 256), 256)
            ob[:, lanes] = jnp.dot(tv[...], fv[:, lanes], preferred_element_type=F32)
            return 0
        lax.fori_loop(0, VIRT // 256, body, 0)

    def dots(c, groups, part=None):
        w = WIDTHS[c]
        size = ROWS // (2 if part is None else PARTS[c])

        def product(rows, h, start, count):
            ks = pl.ds(pl.multiple_of((h * SIDE + start) * SIDE * HALF, SIDE * HALF), count * SIDE * HALF)
            blocks = ts[c][pl.ds((h * SIDE + start) * SIDE, count * SIDE)].reshape(count * SIDE * HALF, w)
            return jnp.dot(xt[rows, ks], blocks, preferred_element_type=F32)

        def body(step, _):
            own = pl.ds(step * size, size)
            rows = pl.ds(pl.multiple_of(step * size * OCC_J, size * OCC_J), size * OCC_J)
            if groups == 0:
                total = jnp.dot(bd[rows, :], mid[:, STARTS[c]:STARTS[c] + w], preferred_element_type=F32)
            else:
                total = accs[c][own].reshape(size * OCC_J, w)
            for h in range(2):
                q, _ = axes(h)
                if groups < 2:
                    total = total + product(rows, h, (q // 2 if groups == 0 else 1 - q // 2) * 2, 2)
                else:
                    total = total + product(rows, h, 3 - q if groups == 2 else (q + 2) % SIDE, 1)
            accs[c][own] = total.reshape(size, SIDE, 2, COLS, w)
            return 0
        if part is None:
            lax.fori_loop(0, 2, body, 0)
        else:
            body(part, 0)

    def share(c, part):
        size = ROWS // PARTS[c]
        return pl.ds(part * size, size)

    def to_sibling(c, part):
        i = share(c, part)
        return pltpu.make_async_remote_copy(
            src_ref=s1s[c].at[i], dst_ref=r1s[c].at[i], send_sem=as_.at[0], recv_sem=ar.at[c + part],
            device_id=sibling, device_id_type=MESH)

    def SA(c, part=0):
        i = share(c, part)
        s1s[c][i] = accs[c][i, :, 1 - core].astype(BF)
        to_sibling(c, part).start()

    def SB(c, part=0):
        w, i = WIDTHS[c], share(c, part)
        cols = pl.ds(STARTS[c], w)
        to_sibling(c, part).wait_recv()
        for d in (2, 1, 3):
            to = (z + d) % SIDE
            s2s[c][d - 1, i] = (accs[c][i, to, core] + r1s[c][i, to].astype(F32)).astype(BF)
            pltpu.make_async_remote_copy(
                src_ref=s2s[c].at[d - 1, i], dst_ref=r2_hbm.at[d - 1, i, :, cols], send_sem=bs.at[0], recv_sem=br.at[0],
                device_id=zdev(d), device_id_type=MESH).start()
        size = ROWS // PARTS[c]
        one = ob[part * size * COLS:(part + 1) * size * COLS, STARTS[c]:STARTS[c] + w].reshape(size, COLS, w)
        finv[i, :, cols] = accs[c][i, z, core] + r1s[c][i, z].astype(F32) + one
        pltpu.make_async_copy(finv.at[i, :, cols], fin_hbm.at[i, :, cols], osem.at[0]).start()

    for name, *args in SCHEDULE:
        dict(load_rest=load_rest, D1=D1, O=O, E1=E1, N=N, E2=E2, G=G, H=H, prep=prep, build=build, middle=middle, onebody=onebody, dots=dots, SA=SA, SB=SB)[name](*args)

    for c in range(n):
        ref = ts[c].at[pl.ds(0, 30)]
        pltpu.make_async_remote_copy(
            src_ref=ref, dst_ref=ref, send_sem=gs.at[c], recv_sem=gr.at[c], device_id=sibling, device_id_type=MESH).wait_send()
    pltpu.make_async_remote_copy(
        src_ref=ts[0], dst_ref=ts[0], send_sem=as_.at[0], recv_sem=ar.at[0], device_id=sibling, device_id_type=MESH).wait_send()
    pltpu.make_async_copy(finv, fin_hbm, osem.at[0]).wait()
    last = pltpu.make_async_remote_copy(
        src_ref=r2_hbm, dst_ref=r2_hbm, send_sem=bs.at[0], recv_sem=br.at[0], device_id=sibling, device_id_type=MESH)
    last.wait_send()
    last.wait_recv()


def local(amplitudes, hole_int, ladder_int, cycle_virt, cycle_occ, irrep_rows, irrep_cols, irrep_virt):
    vm, dma = pltpu.VMEM, pltpu.SemaphoreType.DMA
    any_ = pl.BlockSpec(memory_space=pl.ANY)
    scratch = [
        vm((ROWS * COLS, VIRT), BF), vm((2, SIDE, ROWS, SIDE, HALF, OCC_J), BF), vm((ROWS * OCC_J, OCC_I * COLS), BF),
        vm((VIRT, VIRT), BF), vm((VIRT, VIRT), BF), vm((2, SIDE, SIDE, HALF, OCC_J), BF), vm((OCC_J, OCC_J), jnp.int32),
        vm((VIRT, 128), BF), vm((ROWS * OCC_J, ROWS * COLS), BF), vm((ROWS * COLS, VIRT), BF), vm((ROWS * COLS, VIRT), F32),
        vm((ROWS, COLS, VIRT), F32), vm((OCC_J, OCC_J), BF), vm((1, OCC_J), jnp.int32), vm((1, VIRT), jnp.int32),
        pltpu.SMEM((OCC_I,), jnp.int32),
    ]
    scratch += [vm((2 * SIDE * SIDE, HALF, w), BF) for w in WIDTHS]
    scratch += [vm((ROWS, SIDE, 2, COLS, w), F32) for w in WIDTHS]
    scratch += [vm((ROWS, SIDE, COLS, w), BF) for w in WIDTHS]
    scratch += [vm((ROWS, SIDE, COLS, w), BF) for w in WIDTHS]
    scratch += [vm((SIDE - 1, ROWS, COLS, w), BF) for w in WIDTHS]
    scratch += [dma((k,)) for k in (1, 1, 2, 2, 1, 4, NCH, NCH * EVENTS, 1, NCH + PARTS[-1], 1, 1)]
    own, others = pl.pallas_call(
        kernel,
        out_shape=(jax.ShapeDtypeStruct((ROWS, COLS, VIRT), F32), jax.ShapeDtypeStruct((SIDE - 1, ROWS, COLS, VIRT), BF)),
        in_specs=[any_] * 8,
        out_specs=(any_, any_),
        scratch_shapes=scratch,
        compiler_params=pltpu.CompilerParams(collective_id=0, has_side_effects=True, vmem_limit_bytes=60 * 2**20),
        name="residual",
    )(amplitudes.reshape(ROWS * COLS, VIRT), hole_int.reshape(ROWS, SIDE, SIDE, 2, HALF, OCC_J), ladder_int, cycle_virt,
      cycle_occ, irrep_rows, irrep_cols.reshape(1, OCC_J), irrep_virt.reshape(1, VIRT))
    def final(own_ref, others_ref, out_ref):
        total = own_ref[...]
        for d in range(SIDE - 1):
            total = total + others_ref[d].astype(F32)
        out_ref[...] = total.astype(BF)

    rows = pl.BlockSpec((ROWS // 2, COLS, VIRT), lambda i: (i, 0, 0))
    return pl.pallas_call(
        final,
        grid=(2,),
        out_shape=jax.ShapeDtypeStruct((ROWS, COLS, VIRT), BF),
        in_specs=[rows, pl.BlockSpec((SIDE - 1, ROWS // 2, COLS, VIRT), lambda i: (0, i, 0, 0))],
        out_specs=rows,
        compiler_params=pltpu.CompilerParams(vmem_limit_bytes=60 * 2**20),
        name="final",
    )(own, others)


def solution(mesh):
    placed = (P("row", "col", None), P("row", None, "col", None), P(), P(), P(), P(), P(), P())
    return jax.shard_map(
        local, mesh=mesh, in_specs=placed, out_specs=P("row", "col", None), check_vma=False
    )
```
